128 devices in a mesh: gx: 4 (over x), gy: 32 (over y, z, core).
Axes of the slice: x: 4, y: 4, z: 4, core: 2. Of those that a mesh axis runs over, the one named last changes fastest.
Arguments:
- grid_scalars: float32 [54, 8, 64, 128], P(None, 'gx', 'gy'), may hold values from -6 to 6
- axial_speed: float32 [8, 64, 128], P('gx', 'gy'), may hold values from 0.1 to 0.4
- particles: float32 [54, 32, 65536], P(None, None, ('gx', 'gy')), may hold values from -6 to 6
- cell_owner: int32 [8, 64, 128], P('gx', 'gy'), may hold values from 0 to 31, as said below
- cell_slot: int32 [8, 64, 128], P('gx', 'gy'), may hold values from 0 to 511, as said below
- mix_rate: float32 [65536], P(('gx', 'gy')), may hold values from 0.2 to 0.6
- partner: int32 [32, 65536], P(None, ('gx', 'gy')), may hold values from 0 to 31, as said below
- chem_input: bfloat16 [256, 54], replicated, may hold values from -0.875 to 0.875
- chem_hidden: bfloat16 [256, 256], replicated, may hold values from -0.375 to 0.375
- chem_output: bfloat16 [54, 256], replicated, may hold values from -0.375 to 0.375
- react_slots: int32 [128, 256], P(('gx', 'gy')), may hold values from 0 to 511, as said below
- react_count: int32 [128], P(('gx', 'gy')), may hold values from 1 to 256, as said below
- leave_slots: int32 [128, 256], P(('gx', 'gy')), may hold values from 0 to 512, as said below
- arrive_slots: int32 [128, 256], P(('gx', 'gy')), may hold values from 0 to 512, as said below
Outputs:
- grid_out: float32 [54, 8, 64, 128], P(None, 'gx', 'gy')
- particles_out: float32 [54, 32, 65536], P(None, None, ('gx', 'gy'))
The draws below stay inside these ranges and needn't reach their ends.
Inputs may be any that keep to these rules, and one draw needn't show every extreme that they name: `cell_owner`: within each gx index, each of the 32 owners holds exactly 512 cells of that gx index's grid boxes, each slot once; from one grid box to one owner go at most 24 cells, and exactly 24 for some pairs in every draw. `cell_slot`: slots as described for cell_owner. In each cell partner pairs the 32 particles: partner of partner is the particle itself, never itself. `react_slots`: distinct slots in each owner's row. `react_count`: some owner has 256 live entries in every draw. `leave_slots`: every device hands one or 2 cells to every device, 2 to some; the value 512 marks an empty place; the leaving slots of a device are distinct and are exactly the slots that arriving cells take there. `arrive_slots`: as for leave_slots.
All inputs are finite; a program needn't handle non-finite values.
Results may differ from the reference program's by a relative error of at most 0.0013.
Values sent between devices are 32-bit elements; how exact they have to be, the bound alone decides.
A program may use at most 128 MiB of HBM per device.

```python
import jax
import jax.numpy as jnp
from jax import lax

NS = 54
HID = 256
NP = 32
BX = 2
BY = 2
BZ = 128
SUBSTEPS = 2
CAPM = 2
CDEV = 512
RMAX = 256
NX = 8
NY = 64
NZ = 128
PCELLS = 65536
N_GX = 4
N_GY = 32
DEVICES = 128


def shuffled(key, leading, length):
    scores = jax.random.randint(key, leading + (length,), 0, 1 << 20) * length + jnp.arange(length, dtype=jnp.int32)
    return jnp.argsort(scores, axis=-1).astype(jnp.int32)


def arrange(values):
    return values.reshape(N_GX, N_GY, BX, BY, BZ).transpose(0, 2, 1, 3, 4).reshape(NX, NY, NZ).astype(jnp.int32)


def partition_maps(key):
    base = jax.random.fold_in(key, 7)
    first_key, second_key, third_key = jax.random.split(base, 3)
    share = CDEV // N_GY
    ordering = shuffled(first_key, (N_GX,), N_GY)
    counts = jnp.where(ordering < N_GY // 2, 3 * share // 2, share // 2)
    ending = jnp.cumsum(counts, axis=1)
    within = jnp.arange(CDEV, dtype=jnp.int32)
    offset = jnp.sum((ending[:, None, :] <= within[None, :, None]).astype(jnp.int32), axis=2)
    boxes = jnp.arange(N_GY, dtype=jnp.int32)
    owner_of = (boxes[None, :, None] + offset[:, None, :]) % N_GY
    slot_perm = shuffled(second_key, (N_GX, N_GY), CDEV)
    row_index = jnp.arange(N_GX, dtype=jnp.int32)[:, None, None]
    slot_of = slot_perm.reshape(-1)[(row_index * N_GY + owner_of) * CDEV + within[None, None, :]]
    cell_perm = shuffled(third_key, (N_GX, N_GY), CDEV)
    inverse = jnp.argsort(cell_perm, axis=-1)
    owner_local = jnp.take_along_axis(owner_of, inverse, axis=-1)
    slot_local = jnp.take_along_axis(slot_of, inverse, axis=-1)
    return (arrange(owner_local), arrange(slot_local))


def draw_cell_owner(key, part):
    return partition_maps(key)[0]


def draw_cell_slot(key, part):
    return partition_maps(key)[1]


def migration_lists(key):
    base = jax.random.fold_in(key, 29)
    first_key, second_key, third_key = jax.random.split(base, 3)
    device_ids = jnp.arange(DEVICES, dtype=jnp.int32)
    extra = jax.random.randint(first_key, (DEVICES,), 0, 2)
    forced = jax.random.randint(second_key, (), 0, DEVICES)
    counts = 1 + jnp.maximum(extra, (device_ids == forced).astype(jnp.int32))
    starting = jnp.cumsum(counts) - counts
    leaving = shuffled(third_key, (DEVICES,), CDEV)
    offset = (device_ids[None, :] - device_ids[:, None]) % DEVICES
    send_parts = []
    place_parts = []
    for copy_index in range(CAPM):
        position = starting[offset] + copy_index
        valid = copy_index < counts[offset]
        sending = jnp.take_along_axis(leaving, jnp.clip(position, 0, CDEV - 1), axis=1)
        send_parts.append(jnp.where(valid, sending, CDEV))
        position_back = position.T
        valid_back = valid.T
        placing = jnp.take_along_axis(leaving, jnp.clip(position_back, 0, CDEV - 1), axis=1)
        place_parts.append(jnp.where(valid_back, placing, CDEV))
    send_table = jnp.stack(send_parts, axis=-1).reshape(DEVICES, DEVICES * CAPM).astype(jnp.int32)
    place_table = jnp.stack(place_parts, axis=-1).reshape(DEVICES, DEVICES * CAPM).astype(jnp.int32)
    return (send_table, place_table)


def draw_leave_slots(key, part):
    return migration_lists(key)[0]


def draw_arrive_slots(key, part):
    return migration_lists(key)[1]


def draw_react_slots(key, part):
    return shuffled(jax.random.fold_in(key, 41), (DEVICES,), CDEV)[:, :RMAX]


def draw_react_count(key, part):
    first_key, second_key = jax.random.split(jax.random.fold_in(key, 43))
    counts = jax.random.randint(first_key, (DEVICES,), RMAX // 8, RMAX // 2 + 1)
    forced = jax.random.randint(second_key, (), 0, DEVICES)
    return jnp.where(jnp.arange(DEVICES, dtype=jnp.int32) == forced, RMAX, counts).astype(jnp.int32)


def draw_partner(key, part):
    ordering = shuffled(jax.random.fold_in(key, 53), (PCELLS,), NP)
    inverse = jnp.argsort(ordering, axis=-1).astype(jnp.int32)
    mates = jnp.take_along_axis(ordering, jnp.bitwise_xor(inverse, 1), axis=-1)
    return mates.T.astype(jnp.int32)


def level_of(own_key, shape, shards, least, high):
    level = 1.0
    for dim, blocks in shards:
        steps = jax.random.uniform(jax.random.fold_in(jax.random.fold_in(own_key, 6), dim), (blocks,), jnp.float32, least / len(shards), high / len(shards))
        level = level * jnp.repeat(jnp.exp(steps), shape[dim] // blocks).reshape((-1,) + (1,) * (len(shape) - 1 - dim))
    return level


def scatter_about(stream_key, extent, spread, most, shards=(), kind=jnp.bfloat16):
    drawn = spread * jax.random.normal(stream_key, extent, jnp.float32)
    if shards:
        drawn = drawn * level_of(stream_key, extent, shards, -0.22, 0.18)
    return jnp.clip(drawn, -most, most).astype(kind)


def setup_inputs(seed: int = 0) -> dict:
    splits = jax.random.split(jax.random.key(seed), 15)
    grid_scalars = scatter_about(splits[0], (NS, NX, NY, NZ), 1.0, 6.0, ((1, 4), (2, 32)), jnp.float32)
    axial_speed = jnp.clip(0.1 + 0.3 * jax.random.uniform(splits[1], (NX, NY, NZ), jnp.float32) ** level_of(splits[1], (NX, NY, NZ), ((0, 4), (1, 32)), -0.2, 0.2), 0.1, 0.4)
    particles = scatter_about(splits[2], (NS, NP, PCELLS), 1.0, 6.0, ((2, 128),), jnp.float32)
    cell_owner = draw_cell_owner(jax.random.fold_in(splits[14], 71), 0)
    cell_slot = draw_cell_slot(jax.random.fold_in(splits[14], 71), 0)
    mix_rate = jnp.clip(0.2 + 0.400000021 * jax.random.uniform(splits[5], (PCELLS,), jnp.float32) ** level_of(splits[5], (PCELLS,), ((0, 128),), -0.2, 0.2), 0.2, 0.6)
    partner = draw_partner(jax.random.fold_in(splits[14], 71), 0)
    chem_input = scatter_about(splits[7], (HID, NS), NS ** -0.5, 0.875)
    chem_hidden = scatter_about(splits[8], (HID, HID), HID ** -0.5, 0.375)
    chem_output = scatter_about(splits[9], (NS, HID), HID ** -0.5, 0.375)
    react_slots = draw_react_slots(jax.random.fold_in(splits[14], 71), 0)
    react_count = draw_react_count(jax.random.fold_in(splits[14], 71), 0)
    leave_slots = draw_leave_slots(jax.random.fold_in(splits[14], 71), 0)
    arrive_slots = draw_arrive_slots(jax.random.fold_in(splits[14], 71), 0)
    return dict(grid_scalars=grid_scalars, axial_speed=axial_speed, particles=particles, cell_owner=cell_owner, cell_slot=cell_slot, mix_rate=mix_rate, partner=partner, chem_input=chem_input, chem_hidden=chem_hidden, chem_output=chem_output, react_slots=react_slots, react_count=react_count, leave_slots=leave_slots, arrive_slots=arrive_slots)


DIFFUSION = 0.1
PAIR_WEIGHT = 0.4


def advance(padded, axial_speed):
    center = padded[:, 1:-1, 1:-1, :]
    upstream = padded[:, :-2, 1:-1, :]
    beside = upstream + padded[:, 2:, 1:-1, :]
    beside = beside + padded[:, 1:-1, :-2, :] + padded[:, 1:-1, 2:, :]
    beside = beside + jnp.roll(center, 1, axis=3) + jnp.roll(center, -1, axis=3)
    return center + DIFFUSION * (beside - 6.0 * center) - axial_speed[None] * (center - upstream)


def particle_section(state, filtered, relaxation, partner, chem_input, chem_hidden, chem_output, chosen_slots, live_count):
    state = state + relaxation[None, None, :] * (filtered[:, None, :] - state)
    partner_state = jnp.take_along_axis(state, partner[None, :, :], axis=1)
    state = state + PAIR_WEIGHT * (partner_state - state)
    chosen = jnp.take(state, chosen_slots, axis=2)
    feed_rows = chosen.reshape(chosen.shape[0], -1).astype(jnp.bfloat16)
    layer_one = jax.nn.silu(jnp.dot(chem_input, feed_rows, preferred_element_type=jnp.float32)).astype(jnp.bfloat16)
    layer_two = jax.nn.silu(jnp.dot(chem_hidden, layer_one, preferred_element_type=jnp.float32)).astype(jnp.bfloat16)
    change = jnp.dot(chem_output, layer_two, preferred_element_type=jnp.float32).astype(jnp.bfloat16)
    change = change.reshape(chosen.shape).astype(jnp.float32)
    active = jnp.arange(chosen_slots.shape[0], dtype=jnp.int32) < live_count
    change = jnp.where(active[None, None, :], change, jnp.zeros_like(change))
    state = state.at[:, :, chosen_slots].add(change)
    source = jnp.zeros(filtered.shape, filtered.dtype).at[:, chosen_slots].set(jnp.mean(change, axis=1))
    return state, source


def reference(grid_scalars, axial_speed, particles, cell_owner, cell_slot, mix_rate, partner, chem_input, chem_hidden, chem_output, react_slots, react_count, leave_slots, arrive_slots):
    devices = N_GX * N_GY
    slab_cells = BX * BY * BZ
    row_index = jnp.arange(NX, dtype=jnp.int32)[:, None, None] // BX
    target = ((row_index * N_GY + cell_owner) * slab_cells + cell_slot).reshape(-1).astype(jnp.int32)
    state = particles.reshape(NS, NP, devices, slab_cells).transpose(2, 0, 1, 3)
    relaxation = mix_rate.reshape(devices, slab_cells)
    pairings = partner.reshape(NP, devices, slab_cells).transpose(1, 0, 2)
    grid = grid_scalars
    for substep in range(SUBSTEPS):
        padded = jnp.pad(grid, ((0, 0), (1, 1), (1, 1), (0, 0)))
        grid = advance(padded, axial_speed)
        flattened = grid.reshape(NS, -1)
        filtered = jnp.zeros((NS, devices * slab_cells), grid.dtype).at[:, target].set(flattened)
        filtered = filtered.reshape(NS, devices, slab_cells).transpose(1, 0, 2)

        def per_device(device_index, current=state, values=filtered):
            return particle_section(current[device_index], values[device_index], relaxation[device_index], pairings[device_index], chem_input, chem_hidden, chem_output, react_slots[device_index], react_count[device_index])

        state, source = lax.map(per_device, jnp.arange(devices, dtype=jnp.int32))
        returned = source.transpose(1, 0, 2).reshape(NS, -1)
        grid = grid + jnp.take(returned, target, axis=1).reshape(grid.shape)
    flat_parts = state.reshape(devices, NS * NP, slab_cells)

    def pick(bundle, indices):
        return jnp.take(bundle, indices, axis=1, mode="fill", fill_value=0.0)

    departing = jax.vmap(pick)(flat_parts, leave_slots)
    departing = departing.reshape(devices, NS * NP, devices, CAPM).transpose(2, 1, 0, 3).reshape(devices, NS * NP, devices * CAPM)

    def settle(bundle, arrived, indices):
        return bundle.at[:, indices].set(arrived, mode="drop")

    relocated = jax.vmap(settle)(flat_parts, departing, arrive_slots)
    relocated = relocated.reshape(devices, NS, NP, slab_cells).transpose(1, 2, 0, 3).reshape(NS, NP, devices * slab_cells)
    return grid, relocated
```

```python
import functools

import jax
import jax.numpy as jnp
from jax import lax
from jax.experimental import pallas as pl
from jax.experimental.pallas import tpu as pltpu
from jax.sharding import PartitionSpec as P

F32, BF16 = jnp.float32, jnp.bfloat16
MESH = pl.DeviceIdType.MESH

NS, NP, CELLS = 54, 32, 512
ROWS = NS * NP
OWNERS, GROUPS = 32, 4
HALF = 16
PLACES = 2 * OWNERS * HALF
LIST = 256
LABEL = 54
VMEM_LIMIT = 56 * 1024 * 1024
NT = (((1,), (1,)), ((), ()))


def split(x):
    hi = x.astype(BF16)
    return hi, (x - hi.astype(F32)).astype(BF16)


def mat(a, b):
    return jnp.dot(a, b, preferred_element_type=F32)


def mat_nt(a, b):
    return lax.dot_general(a, b, NT, preferred_element_type=F32)


def silu(a):
    h = 0.5 * a
    return (h + h * jnp.tanh(h)).astype(BF16)


def packed(picker, values):
    hi, lo = split(values)
    both = mat_nt(picker, jnp.concatenate([hi, lo], axis=0))
    both = both + pltpu.roll(both, 64, axis=1)
    lane = lax.broadcasted_iota(jnp.int32, (PLACES // 2, 128), 1)
    return jnp.where(lane < 64, both[: PLACES // 2], both[PLACES // 2 :])


def unpacked(message, placer):
    turned = message.T
    values = jnp.concatenate([turned[:64], turned[64:]], axis=1)
    hi, lo = split(values)
    both = mat(jnp.concatenate([hi, lo], axis=0), placer)
    return both[:64] + both[64:]


def step_kernel(
    grid_in, speed, parts_in, owner, slot, rate, partner, w_in, w_hid, w_out, listed, count, leave,
    grid_out, parts_out, moving,
    state, faces, halo, f_send, f_recv, s_send, s_recv, to_box, to_slot, reacting, feed, r_f, wi, wo,
    load_sem, store_sem, halo_send, halo_recv, fs_sem, fr_sem, ss_sem, sr_sem,
):
    gx, gy = lax.axis_index("gx"), lax.axis_index("gy")
    barrier = pltpu.get_barrier_semaphore()

    loads = [
        pltpu.make_async_copy(parts_in.at[:, pl.ds(128 * lb, 128)], state.at[lb], load_sem.at[lb]) for lb in range(4)
    ]
    stores = [
        pltpu.make_async_copy(state.at[lb], parts_out.at[:, pl.ds(128 * lb, 128)], store_sem.at[lb]) for lb in range(4)
    ]
    for copy in loads:
        copy.start()

    def greet(k, carry):
        pl.semaphore_signal(barrier, inc=1, device_id={"gy": lax.rem(gy + k, OWNERS)}, device_id_type=MESH)
        return carry

    lax.fori_loop(1, OWNERS, greet, 0)
    for d in (1, GROUPS - 1):
        pl.semaphore_signal(barrier, inc=1, device_id={"gx": lax.rem(gx + d, GROUPS)}, device_id_type=MESH)

    for q in range(4):
        faces[0, q // 2, q % 2, 0:NS, :] = grid_in[pl.ds(q, NS, stride=4), :]
        faces[0, q // 2, q % 2, NS:56, :] = jnp.zeros((56 - NS, 128), F32)

    pl.semaphore_wait(barrier, OWNERS - 1 + 2)

    def halo_copies(t):
        ahead = [
            (faces.at[t, 1], {"gx": lax.rem(gx + 1, GROUPS)}),
            (faces.at[t, 0], {"gx": lax.rem(gx + GROUPS - 1, GROUPS)}),
            (faces.at[t, :, 1], {"gy": lax.rem(gy + 1, OWNERS)}),
            (faces.at[t, :, 0], {"gy": lax.rem(gy + OWNERS - 1, OWNERS)}),
        ]
        return [
            pltpu.make_async_remote_copy(
                src_ref=source,
                dst_ref=halo.at[t, i],
                send_sem=halo_send.at[t, i],
                recv_sem=halo_recv.at[t, i],
                device_id=device,
                device_id_type=MESH,
            )
            for i, (source, device) in enumerate(ahead)
        ]

    def exchange(out, into, t, send_sem, recv_sem):
        def send(k, carry):
            other = lax.rem(gy + k, OWNERS)
            pltpu.make_async_remote_copy(
                src_ref=out.at[t, other],
                dst_ref=into.at[t, gy],
                send_sem=send_sem.at[t],
                recv_sem=recv_sem.at[t],
                device_id={"gy": other},
                device_id_type=MESH,
            ).start()
            return carry

        lax.fori_loop(1, OWNERS, send, 0)
        into[t, gy] = out[t, gy]

    def await_all(buf, t, sem):
        part = buf.at[t, pl.ds(0, OWNERS - 1)]
        pltpu.make_async_copy(part, part, sem.at[t]).wait()

    halos = [halo_copies(t) for t in range(2)]
    for copy in halos[0]:
        copy.start()

    owner_row = jnp.concatenate([owner[q : q + 1, :] for q in range(4)], axis=1)
    label_row = jnp.concatenate([slot[q : q + 1, :] for q in range(4)], axis=1).astype(F32) + 1.0
    mine = (lax.broadcasted_iota(jnp.int32, (OWNERS, CELLS), 0) == owner_row).astype(F32)
    before = (
        lax.broadcasted_iota(jnp.int32, (CELLS, CELLS), 0) < lax.broadcasted_iota(jnp.int32, (CELLS, CELLS), 1)
    ).astype(F32)
    ahead = mat(mine.astype(BF16), before.astype(BF16))
    rank = jnp.sum(mine * ahead, axis=0, keepdims=True)
    place = owner_row.astype(F32) * HALF + rank + jnp.where(rank >= HALF, float(PLACES // 2 - HALF), 0.0)
    place = place.astype(jnp.int32)
    to_box[...] = (lax.broadcasted_iota(jnp.int32, (PLACES, CELLS), 0) == place).astype(F32).astype(BF16)
    live = lax.broadcasted_iota(jnp.int32, (1, LIST), 1) < count[...]
    react_row = jnp.where(live, listed[...], CELLS)
    reacting[...] = (lax.broadcasted_iota(jnp.int32, (CELLS, LIST), 0) == react_row).astype(F32).astype(BF16)
    wi[...] = jnp.zeros_like(wi)
    wi[:, 0:NS] = w_in[...].astype(F32)
    wo[...] = jnp.zeros_like(wo)
    wo[0:NS, :] = w_out[...].astype(F32)
    feed[...] = jnp.zeros_like(feed)

    def mix():
        for lb in range(4):
            cols = slice(128 * lb, 128 * lb + 128)
            mates = [partner[8 * o : 8 * o + 8, cols] for o in range(4)]
            index = [m & 7 for m in mates]
            group = [m >> 3 for m in mates]

            def body(s, carry):
                base = pl.multiple_of(s * NP, NP)
                tiles = [state[lb, pl.ds(base + 8 * g, 8), :] for g in range(4)]
                for o in range(4):
                    mate = jnp.take_along_axis(tiles[0], index[o], axis=0, mode="promise_in_bounds")
                    for g in range(1, 4):
                        other = jnp.take_along_axis(tiles[g], index[o], axis=0, mode="promise_in_bounds")
                        mate = jnp.where(group[o] == g, other, mate)
                    state[lb, pl.ds(base + 8 * o, 8), :] = 0.6 * tiles[o] + 0.4 * mate
                return carry

            lax.fori_loop(0, NS, body, 0)

    def transport(t):
        x_low = jnp.where(gx > 0, 1.0, 0.0).astype(F32)
        x_high = jnp.where(gx < GROUPS - 1, 1.0, 0.0).astype(F32)
        y_low = jnp.where(gy > 0, 1.0, 0.0).astype(F32)
        y_high = jnp.where(gy < OWNERS - 1, 1.0, 0.0).astype(F32)
        made = []
        for x in range(2):
            for y in range(2):
                center = faces[t, x, y]
                up = faces[t, 0, y] if x else halo[t, 0, y] * x_low
                down = halo[t, 1, y] * x_high if x else faces[t, 1, y]
                left = faces[t, x, 0] if y else halo[t, 2, x] * y_low
                right = halo[t, 3, x] * y_high if y else faces[t, x, 1]
                around = up + down + left + right
                around = around + pltpu.roll(center, 1, axis=1) + pltpu.roll(center, 127, axis=1)
                q = 2 * x + y
                made.append(center + 0.1 * (around - 6.0 * center) - speed[q : q + 1, :] * (center - up))
        return jnp.concatenate(made, axis=1)

    rate_row = rate[...]
    keep_row = 1.0 - rate_row

    def chemistry(t):
        weights_in = wi[...].astype(BF16)
        weights_hid = w_hid[...]
        weights_out = wo[...].astype(BF16)

        def body(g, total):
            for i in range(4):
                own = jnp.concatenate(
                    [state[lb, pl.ds(4 * g + i, NS, stride=NP), :] for lb in range(4)], axis=1
                )
                feed[64 * i : 64 * i + NS, :] = own * keep_row + r_f[0:NS, :]
            chosen = mat(feed[...].astype(BF16), reacting[...]).astype(BF16)
            columns = jnp.concatenate([chosen[64 * i : 64 * i + 64] for i in range(4)], axis=1)
            one = silu(mat(weights_in, columns))
            two = silu(mat(weights_hid, one))
            change = mat(weights_out, two).astype(BF16)
            parts = [change[:, LIST * i : LIST * i + LIST] for i in range(4)]
            back = mat_nt(jnp.concatenate(parts, axis=0), reacting[...])
            for i in range(4):
                made = feed[64 * i : 64 * i + NS, :] + back[64 * i : 64 * i + NS, :]
                for lb in range(4):
                    state[lb, pl.ds(4 * g + i, NS, stride=NP), :] = made[:, 128 * lb : 128 * lb + 128]
                total = total + parts[i].astype(F32)
            return total

        total = lax.fori_loop(0, NP // 4, body, jnp.zeros((64, LIST), F32))
        hi, lo = split(total * (1.0 / NP))
        both = mat_nt(jnp.concatenate([hi, lo], axis=0), reacting[...])
        return both[:64] + both[64:]

    row = lax.broadcasted_iota(jnp.int32, (64, CELLS), 0)
    for t in range(2):
        for copy in halos[t]:
            copy.wait_recv()
        grid = jnp.concatenate([transport(t), jnp.zeros((8, CELLS), F32)], axis=0)
        message = packed(to_box[...], jnp.where(row == LABEL, label_row, grid))
        for j in range(OWNERS):
            f_send[t, j] = message[HALF * j : HALF * j + HALF]
        exchange(f_send, f_recv, t, fs_sem, fr_sem)
        if t == 0:
            for copy in loads:
                copy.wait()
        mix()
        await_all(f_recv, t, fr_sem)
        arrived = f_recv[t].reshape(PLACES // 2, 128)
        if t == 0:
            lane = lax.broadcasted_iota(jnp.int32, (PLACES // 2, CELLS), 1).astype(F32) + 1.0
            for h in range(2):
                labels = arrived[:, 64 * h + LABEL : 64 * h + LABEL + 1]
                to_slot[h * PLACES // 2 : (h + 1) * PLACES // 2, :] = (labels == lane).astype(F32).astype(BF16)
        r_f[...] = unpacked(arrived, to_slot[...]) * rate_row
        source = chemistry(t)
        message = packed(to_slot[...], source)
        for j in range(OWNERS):
            s_send[t, j] = message[HALF * j : HALF * j + HALF]
        exchange(s_send, s_recv, t, ss_sem, sr_sem)
        if t == 1:
            for copy in stores:
                copy.start()
            goes = (lax.broadcasted_iota(jnp.int32, (CELLS, LIST), 0) == leave[...]).astype(F32)
            goes = goes.T.astype(BF16)
            for j in range(14):
                size = min(128, ROWS - 128 * j)
                block = [state[lb, 128 * j : 128 * j + size, :] for lb in range(4)]
                hi, lo = split(jnp.concatenate(block, axis=1))
                moving[:, j, 0:size] = mat_nt(goes, hi) + mat_nt(goes, lo)
            moving[:, 13, 64:128] = jnp.zeros((LIST, 64), F32)
        await_all(s_recv, t, sr_sem)
        grid = grid + unpacked(s_recv[t].reshape(PLACES // 2, 128), to_box[...])
        if t == 0:
            for q in range(4):
                faces[1, q // 2, q % 2] = grid[0:56, 128 * q : 128 * q + 128]
            for copy in halos[1]:
                copy.start()
        else:
            for q in range(4):
                grid_out[pl.ds(q, NS, stride=4), :] = grid[0:NS, 128 * q : 128 * q + 128]
    for copy in stores:
        copy.wait()
    for t in range(2):
        for copy in halos[t]:
            copy.wait_send()
        await_all(f_send, t, fs_sem)
        await_all(s_send, t, ss_sem)


def settle_kernel(parts_in, arrived, arrive, parts_out, state, load_sem, store_sem):
    def span(j):
        return pl.ds(128 * j, min(128, ROWS - 128 * j))

    loads = [pltpu.make_async_copy(parts_in.at[span(j)], state.at[span(j)], load_sem.at[j]) for j in range(14)]
    stores = [pltpu.make_async_copy(state.at[span(j)], parts_out.at[span(j)], store_sem.at[j]) for j in range(14)]
    for copy in loads:
        copy.start()
    lands = (lax.broadcasted_iota(jnp.int32, (CELLS, LIST), 0) == arrive[...]).astype(F32).astype(BF16)
    taken = mat_nt(jnp.ones((8, LIST), BF16), lands)[0:1]
    for j in range(14):
        size = min(128, ROWS - 128 * j)
        hi, lo = split(arrived[:, j, :].T)
        moved = mat_nt(hi, lands) + mat_nt(lo, lands)
        loads[j].wait()
        kept = state[128 * j : 128 * j + size, :]
        state[128 * j : 128 * j + size, :] = jnp.where(taken > 0.5, moved[0:size], kept)
        stores[j].start()
    for copy in stores:
        copy.wait()


def per_device(
    grid_scalars, axial_speed, particles, cell_owner, cell_slot, mix_rate, partner,
    chem_input, chem_hidden, chem_output, react_slots, react_count, leave_slots, arrive_slots,
):
    vmem = pl.BlockSpec(memory_space=pltpu.VMEM)
    hbm = pl.BlockSpec(memory_space=pl.ANY)
    dma = pltpu.SemaphoreType.DMA
    messages = pltpu.VMEM((2, OWNERS, HALF, 128), F32)
    grid, parts, moving = pl.pallas_call(
        step_kernel,
        out_shape=(
            jax.ShapeDtypeStruct((4 * NS, 128), F32),
            jax.ShapeDtypeStruct((ROWS, CELLS), F32),
            jax.ShapeDtypeStruct((LIST, 14, 128), F32),
        ),
        in_specs=[vmem, vmem, hbm] + [vmem] * 10,
        out_specs=(vmem, hbm, vmem),
        scratch_shapes=[
            pltpu.VMEM((4, ROWS, 128), F32),
            pltpu.VMEM((2, 2, 2, 56, 128), F32),
            pltpu.VMEM((2, 4, 2, 56, 128), F32),
            messages,
            messages,
            messages,
            messages,
            pltpu.VMEM((PLACES, CELLS), BF16),
            pltpu.VMEM((PLACES, CELLS), BF16),
            pltpu.VMEM((CELLS, LIST), BF16),
            pltpu.VMEM((256, CELLS), F32),
            pltpu.VMEM((64, CELLS), F32),
            pltpu.VMEM((256, 64), F32),
            pltpu.VMEM((64, 256), F32),
            dma((4,)),
            dma((4,)),
            dma((2, 4)),
            dma((2, 4)),
            dma((2,)),
            dma((2,)),
            dma((2,)),
            dma((2,)),
        ],
        compiler_params=pltpu.CompilerParams(
            collective_id=0, has_side_effects=True, vmem_limit_bytes=VMEM_LIMIT
        ),
        name="step",
    )(
        grid_scalars.reshape(4 * NS, 128),
        axial_speed.reshape(4, 128),
        particles.reshape(ROWS, CELLS),
        cell_owner.reshape(4, 128),
        cell_slot.reshape(4, 128),
        mix_rate.reshape(1, CELLS),
        partner,
        chem_input,
        chem_hidden,
        chem_output,
        react_slots,
        react_count.reshape(1, 1),
        leave_slots,
    )
    arrived = lax.all_to_all(moving.reshape(128, 2, 14, 128), ("gx", "gy"), 0, 0, tiled=True)
    out = pl.pallas_call(
        settle_kernel,
        out_shape=jax.ShapeDtypeStruct((ROWS, CELLS), F32),
        in_specs=[hbm, vmem, vmem],
        out_specs=hbm,
        scratch_shapes=[pltpu.VMEM((ROWS, CELLS), F32), dma((14,)), dma((14,))],
        compiler_params=pltpu.CompilerParams(vmem_limit_bytes=VMEM_LIMIT),
        name="settle",
    )(parts, arrived.reshape(LIST, 14, 128), arrive_slots)
    return grid.reshape(grid_scalars.shape), out.reshape(particles.shape)


def solution(mesh):
    placed = (
        P(None, "gx", "gy", None),
        P("gx", "gy", None),
        P(None, None, ("gx", "gy")),
        P("gx", "gy", None),
        P("gx", "gy", None),
        P(("gx", "gy")),
        P(None, ("gx", "gy")),
        P(),
        P(),
        P(),
        P(("gx", "gy"), None),
        P(("gx", "gy")),
        P(("gx", "gy"), None),
        P(("gx", "gy"), None),
    )
    return jax.shard_map(
        per_device,
        mesh=mesh,
        in_specs=placed,
        out_specs=(P(None, "gx", "gy", None), P(None, None, ("gx", "gy"))),
        check_vma=False,
    )
```

```python
import functools

import jax
import jax.numpy as jnp
from jax import lax
from jax.experimental import pallas as pl
from jax.experimental.pallas import tpu as pltpu
from jax.sharding import PartitionSpec as P

F32, BF16 = jnp.float32, jnp.bfloat16
MESH = pl.DeviceIdType.MESH

NS, NP, CELLS = 54, 32, 512
ROWS = NS * NP
OWNERS, GROUPS, DEVICES = 32, 4, 128
HALF = 16
PLACES = 2 * OWNERS * HALF
LIST = 256
SPAN = 432
CHAINS, WIDE = 2, 4
LABEL = 54
VMEM_LIMIT = 56 * 1024 * 1024
NT = (((1,), (1,)), ((), ()))


def split(x):
    hi = x.astype(BF16)
    return hi, (x - hi.astype(F32)).astype(BF16)


def mat(a, b):
    return jnp.dot(a, b, preferred_element_type=F32)


def mat_nt(a, b):
    return lax.dot_general(a, b, NT, preferred_element_type=F32)


def silu(a):
    h = 0.5 * a
    return (h + h * jnp.tanh(h)).astype(BF16)


def packed(picker, values):
    hi, lo = split(values)
    both = mat_nt(picker, jnp.concatenate([hi, lo], axis=0))
    both = both + pltpu.roll(both, 64, axis=1)
    lane = lax.broadcasted_iota(jnp.int32, (PLACES // 2, 128), 1)
    return jnp.where(lane < 64, both[: PLACES // 2], both[PLACES // 2 :])


def unpacked(message, placer):
    turned = message.T
    values = jnp.concatenate([turned[:64], turned[64:]], axis=1)
    hi, lo = split(values)
    both = mat(jnp.concatenate([hi, lo], axis=0), placer)
    return both[:64] + both[64:]


def step_kernel(
    grid_in, speed, parts_in, owner, slot, rate, partner, w_in, w_hid, w_out, listed, count, leave, arrive,
    grid_out, parts_out,
    state, guest, faces, halo, f_send, f_recv, s_send, s_recv, moving, moved, r_moving, r_moved,
    to_box, to_slot, order, final, turn, mates, feed, r_f, r_late, r_g, made, wi, wo,
    load_sem, store_sem, halo_send, halo_recv, fs_sem, fr_sem, ss_sem, sr_sem, move_send, move_recv,
):
    gx, gy = lax.axis_index("gx"), lax.axis_index("gy")
    me = gx * OWNERS + gy
    barrier = pltpu.get_barrier_semaphore()

    loads = [
        pltpu.make_async_copy(parts_in.at[:, pl.ds(128 * lb, 128)], state.at[lb], load_sem.at[lb]) for lb in range(4)
    ]
    for copy in loads:
        copy.start()

    def device(k):
        other = lax.rem(me + k, DEVICES)
        return other, {"gx": other // OWNERS, "gy": lax.rem(other, OWNERS)}

    def greet(k, carry):
        pl.semaphore_signal(barrier, inc=1, device_id=device(k)[1], device_id_type=MESH)
        return carry

    lax.fori_loop(1, DEVICES, greet, 0)

    for q in range(4):
        faces[0, q // 2, q % 2, 0:NS, :] = grid_in[pl.ds(q, NS, stride=4), :]
        faces[0, q // 2, q % 2, NS:56, :] = jnp.zeros((56 - NS, 128), F32)

    pl.semaphore_wait(barrier, DEVICES - 1)

    def halo_copies(t):
        ahead = [
            (faces.at[t, 1], {"gx": lax.rem(gx + 1, GROUPS)}),
            (faces.at[t, 0], {"gx": lax.rem(gx + GROUPS - 1, GROUPS)}),
            (faces.at[t, :, 1], {"gy": lax.rem(gy + 1, OWNERS)}),
            (faces.at[t, :, 0], {"gy": lax.rem(gy + OWNERS - 1, OWNERS)}),
        ]
        return [
            pltpu.make_async_remote_copy(
                src_ref=source,
                dst_ref=halo.at[t, i],
                send_sem=halo_send.at[t, i],
                recv_sem=halo_recv.at[t, i],
                device_id=device,
                device_id_type=MESH,
            )
            for i, (source, device) in enumerate(ahead)
        ]

    def exchange(out, into, t, send_sem, recv_sem):
        def send(k, carry):
            other = lax.rem(gy + k, OWNERS)
            pltpu.make_async_remote_copy(
                src_ref=out.at[t, other],
                dst_ref=into.at[t, gy],
                send_sem=send_sem.at[t],
                recv_sem=recv_sem.at[t],
                device_id={"gy": other},
                device_id_type=MESH,
            ).start()
            return carry

        lax.fori_loop(1, OWNERS, send, 0)
        into[t, gy] = out[t, gy]

    def exchange_all(out, into, i):
        def send(k, carry):
            other, where = device(k)
            pltpu.make_async_remote_copy(
                src_ref=out.at[other],
                dst_ref=into.at[me],
                send_sem=move_send.at[i],
                recv_sem=move_recv.at[i],
                device_id=where,
                device_id_type=MESH,
            ).start()
            return carry

        lax.fori_loop(1, DEVICES, send, 0)
        into[me] = out[me]

    def await_all(part, sem):
        pltpu.make_async_copy(part, part, sem).wait()

    def await_row(buf, t, sem):
        await_all(buf.at[t, pl.ds(0, OWNERS - 1)], sem.at[t])

    halos = [halo_copies(t) for t in range(2)]
    for copy in halos[0]:
        copy.start()

    def iota(shape, dim):
        return lax.broadcasted_iota(jnp.int32, shape, dim)

    owner_row = jnp.concatenate([owner[q : q + 1, :] for q in range(4)], axis=1)
    label_row = jnp.concatenate([slot[q : q + 1, :] for q in range(4)], axis=1).astype(F32) + 1.0
    mine = (iota((OWNERS, CELLS), 0) == owner_row).astype(F32)
    before = (iota((CELLS, CELLS), 0) < iota((CELLS, CELLS), 1)).astype(F32)
    ahead = mat(mine.astype(BF16), before.astype(BF16))
    rank = jnp.sum(mine * ahead, axis=0, keepdims=True)
    place = owner_row.astype(F32) * HALF + rank + jnp.where(rank >= HALF, float(PLACES // 2 - HALF), 0.0)
    place = place.astype(jnp.int32)
    to_box[...] = (iota((PLACES, CELLS), 0) == place).astype(F32).astype(BF16)
    picks = (iota((CELLS, LIST), 0) == listed[...]).astype(F32)
    others = 1.0 - mat(picks.astype(BF16), jnp.ones((LIST, 128), BF16))
    later = (iota((CELLS, CELLS), 1) < iota((CELLS, CELLS), 0)).astype(F32)
    column = mat(later.astype(BF16), others.astype(BF16))
    column = jnp.where(others > 0.5, column, -1.0)[:, 0:1]
    rest = (column == iota((CELLS, LIST), 1).astype(F32)).astype(F32)
    chosen = jnp.concatenate([picks, rest], axis=1)
    order[...] = chosen.astype(BF16)
    live_row = (iota((1, LIST), 1) < count[...]).astype(F32)
    wi[...] = jnp.zeros_like(wi)
    wi[0:NS, :] = w_in[...].astype(F32)
    wo[...] = jnp.zeros_like(wo)
    wo[0:NS, :] = w_out[...].astype(F32)
    feed[...] = jnp.zeros_like(feed)
    weights_in = wi[...].T[:, 0:64].astype(BF16)
    weights_out = wo[...].astype(BF16)
    mates[0] = partner[...]

    def mix(t, keep_row):
        for lb in range(4):
            cols = slice(128 * lb, 128 * lb + 128)
            index = [mates[t, 8 * o : 8 * o + 8, cols] & 7 for o in range(4)]
            group = [mates[t, 8 * o : 8 * o + 8, cols] >> 3 for o in range(4)]
            late = t == 1 and lb >= 2

            def body(s, carry):
                base = pl.multiple_of(s * NP, NP)
                tiles = [state[lb, pl.ds(base + 8 * g, 8), :] for g in range(4)]
                for o in range(4):
                    mate = jnp.take_along_axis(tiles[0], index[o], axis=0, mode="promise_in_bounds")
                    for g in range(1, 4):
                        other = jnp.take_along_axis(tiles[g], index[o], axis=0, mode="promise_in_bounds")
                        mate = jnp.where(group[o] == g, other, mate)
                    mixed = 0.6 * tiles[o] + 0.4 * mate
                    if late:
                        mixed = mixed * keep_row[:, cols] + r_late[lb - 2, pl.ds(s, 1), :]
                    state[lb, pl.ds(base + 8 * o, 8), :] = mixed
                return carry

            lax.fori_loop(0, NS, body, 0, unroll=2)

    def rows_of(ref, blocks, start, size):
        return jnp.concatenate([ref[lb, start : start + size, :] for lb in range(blocks)], axis=1)

    def permute():
        for k in range(ROWS // SPAN):
            hi, lo = split(rows_of(state, 4, SPAN * k, SPAN))
            turned = mat(hi, order[...]) + mat(lo, order[...])
            for lb in range(4):
                state[lb, SPAN * k : SPAN * k + SPAN, :] = turned[:, 128 * lb : 128 * lb + 128]

    def transport(t):
        x_low = jnp.where(gx > 0, 1.0, 0.0).astype(F32)
        x_high = jnp.where(gx < GROUPS - 1, 1.0, 0.0).astype(F32)
        y_low = jnp.where(gy > 0, 1.0, 0.0).astype(F32)
        y_high = jnp.where(gy < OWNERS - 1, 1.0, 0.0).astype(F32)
        done = []
        for x in range(2):
            for y in range(2):
                center = faces[t, x, y]
                up = faces[t, 0, y] if x else halo[t, 0, y] * x_low
                down = halo[t, 1, y] * x_high if x else faces[t, 1, y]
                left = faces[t, x, 0] if y else halo[t, 2, x] * y_low
                right = halo[t, 3, x] * y_high if y else faces[t, x, 1]
                around = up + down + left + right
                around = around + pltpu.roll(center, 1, axis=1) + pltpu.roll(center, 127, axis=1)
                q = 2 * x + y
                done.append(center + 0.1 * (around - 6.0 * center) - speed[q : q + 1, :] * (center - up))
        return jnp.concatenate(done, axis=1)

    def chemistry(ref, keep, source, live):
        def body(g, total):
            for c in range(CHAINS):
                for i in range(WIDE):
                    p = (CHAINS * g + c) * WIDE + i
                    own = jnp.concatenate([ref[lb, pl.ds(p, NS, stride=NP), :] for lb in range(2)], axis=1)
                    feed[c * WIDE + i, 0:NS, :] = own * keep + source[0:NS, 0:LIST]
            columns = [
                jnp.concatenate(
                    [jnp.where(live > 0.5, feed[c * WIDE + i], 0.0).astype(BF16) for i in range(WIDE)], axis=1
                )
                for c in range(CHAINS)
            ]
            one = [silu(mat(weights_in, x)) for x in columns]
            two = [silu(mat(w_hid[...], x)) for x in one]
            change = [mat(weights_out, x).astype(BF16).astype(F32) for x in two]
            for c in range(CHAINS):
                for i in range(WIDE):
                    p = (CHAINS * g + c) * WIDE + i
                    part = jnp.where(live > 0.5, change[c][:, LIST * i : LIST * i + LIST], 0.0)
                    done = feed[c * WIDE + i] + part
                    for lb in range(2):
                        ref[lb, pl.ds(p, NS, stride=NP), :] = done[0:NS, 128 * lb : 128 * lb + 128]
                    total = total + part
            return total

        return lax.fori_loop(0, NP // (CHAINS * WIDE), body, jnp.zeros((64, LIST), F32))

    def through(values, matrix, product=mat):
        hi, lo = split(values)
        both = product(jnp.concatenate([hi, lo], axis=0), matrix)
        return both[: values.shape[0]] + both[values.shape[0] :]

    row = iota((64, CELLS), 0)
    for t in range(2):
        for copy in halos[t]:
            copy.wait_recv()
        grid = jnp.concatenate([transport(t), jnp.zeros((8, CELLS), F32)], axis=0)
        message = packed(to_box[...], jnp.where(row == LABEL, label_row, grid))
        for j in range(OWNERS):
            f_send[t, j] = message[HALF * j : HALF * j + HALF]
        exchange(f_send, f_recv, t, fs_sem, fr_sem)
        if t == 0:
            for copy in loads:
                copy.wait()
            mix(0, None)
            permute()
            mates[1] = mat(partner[...].astype(F32).astype(BF16), order[...]).astype(jnp.int32)
            rate_row = through(jnp.broadcast_to(rate[...], (8, CELLS)), order[...])[0:1]
            keep_row = 1.0 - rate_row
            goes = (iota((CELLS, LIST), 0) == leave[...]).astype(F32)
            goes = mat(goes.T.astype(BF16), order[...])
            for lb in range(4):
                turn[lb] = goes[:, 128 * lb : 128 * lb + 128]
            halves = [
                jnp.concatenate([turn[lb, pl.ds(c, DEVICES, stride=2), :] for lb in range(4)], axis=1) for c in range(2)
            ]
            goes_halves = jnp.concatenate(halves, axis=0).astype(BF16)
            goes = goes.astype(BF16)
            lands = (iota((CELLS, LIST), 0) == arrive[...]).astype(F32)
            taken = mat_nt(jnp.ones((8, LIST), BF16), lands.astype(BF16))[0:1]
            lands = lands.T
            for lb in range(4):
                turn[lb] = lands[:, 128 * lb : 128 * lb + 128]
            final[0:CELLS, :] = jnp.where(taken > 0.5, 0.0, chosen.T).astype(BF16)
            for c in range(2):
                final[CELLS + DEVICES * c : CELLS + DEVICES * (c + 1), :] = jnp.concatenate(
                    [turn[lb, pl.ds(c, DEVICES, stride=2), :] for lb in range(4)], axis=1
                ).astype(BF16)
        await_row(f_recv, t, fr_sem)
        arrived = f_recv[t].reshape(PLACES // 2, 128)
        if t == 0:
            lane = iota((PLACES // 2, CELLS), 1).astype(F32) + 1.0
            for h in range(2):
                labels = arrived[:, 64 * h + LABEL : 64 * h + LABEL + 1]
                to_slot[h * PLACES // 2 : (h + 1) * PLACES // 2, :] = (labels == lane).astype(F32).astype(BF16)
        r_f[...] = through(unpacked(arrived, to_slot[...]), order[...]) * rate_row
        for lb in range(2):
            r_late[lb] = r_f[:, LIST + 128 * lb : LIST + 128 * lb + 128]
        if t == 1:
            hi, lo = split(r_f[...])
            both = mat_nt(goes_halves, jnp.concatenate([hi, lo], axis=0))
            both = both + pltpu.roll(both, 64, axis=1)
            r_moving[:, 0, :] = jnp.where(iota((DEVICES, 128), 1) < 64, both[:DEVICES], both[DEVICES:])
            exchange_all(r_moving, r_moved, 1)
        total = chemistry(state, keep_row[:, 0:LIST], r_f, live_row)
        source = through(total * (1.0 / NP), order[:, 0:LIST], mat_nt)
        message = packed(to_slot[...], source)
        for j in range(OWNERS):
            s_send[t, j] = message[HALF * j : HALF * j + HALF]
        exchange(s_send, s_recv, t, ss_sem, sr_sem)
        if t == 0:
            mix(1, keep_row)
            for j in range(13):
                hi, lo = split(rows_of(state, 4, 128 * j, 128))
                value = mat_nt(goes, hi) + mat_nt(goes, lo)
                moving[:, :, j, :] = value.reshape(DEVICES, 2, 128)
            live_all = jnp.concatenate([live_row, jnp.zeros((1, LIST), F32)], axis=1)
            extra = jnp.where(row == 0, rate_row, jnp.where(row == 1, live_all, 0.0))
            hi, lo = split(jnp.concatenate([rows_of(state, 4, 1664, 64), extra], axis=0))
            value = mat_nt(goes, hi) + mat_nt(goes, lo)
            moving[:, :, 13, :] = value.reshape(DEVICES, 2, 128)
            exchange_all(moving, moved, 0)
        else:
            await_all(moved.at[pl.ds(0, DEVICES - 1)], move_recv.at[0])
            await_all(r_moved.at[pl.ds(0, DEVICES - 1)], move_recv.at[1])
            metas = []
            for c in range(2):
                for j in range(14):
                    block = moved[:, c, j, :].T
                    size = min(128, ROWS - 128 * j)
                    guest[c, 128 * j : 128 * j + size, :] = block[0:size]
                metas.append(block[64:72])
            metas = jnp.concatenate(metas, axis=1)
            r_turned = r_moved[...].reshape(DEVICES, 128).T
            r_g[...] = jnp.concatenate([r_turned[0:64], r_turned[64:128]], axis=1)
            chemistry(guest, 1.0 - metas[0:1], r_g, metas[1:2])

            def relax(s, carry):
                base = pl.multiple_of(s * NP, NP)
                for lb in range(2, 4):
                    cols = slice(128 * lb, 128 * lb + 128)
                    span = pl.ds(base, NP)
                    state[lb, span, :] = state[lb, span, :] * keep_row[:, cols] + r_late[lb - 2, pl.ds(s, 1), :]
                return carry

            lax.fori_loop(0, NS, relax, 0)
            stores = [
                pltpu.make_async_copy(
                    made.at[pl.ds(SPAN * k, SPAN)], parts_out.at[pl.ds(SPAN * k, SPAN)], store_sem.at[k]
                )
                for k in range(ROWS // SPAN)
            ]
            for k in range(ROWS // SPAN):
                block = [rows_of(state, 4, SPAN * k, SPAN), rows_of(guest, 2, SPAN * k, SPAN)]
                hi, lo = split(jnp.concatenate(block, axis=1))
                made[SPAN * k : SPAN * k + SPAN, :] = mat(hi, final[...]) + mat(lo, final[...])
                stores[k].start()
        await_row(s_recv, t, sr_sem)
        grid = grid + unpacked(s_recv[t].reshape(PLACES // 2, 128), to_box[...])
        if t == 0:
            for q in range(4):
                faces[1, q // 2, q % 2] = grid[0:56, 128 * q : 128 * q + 128]
            for copy in halos[1]:
                copy.start()
        else:
            for q in range(4):
                grid_out[pl.ds(q, NS, stride=4), :] = grid[0:NS, 128 * q : 128 * q + 128]
    for copy in stores:
        copy.wait()
    for t in range(2):
        for copy in halos[t]:
            copy.wait_send()
        await_row(f_send, t, fs_sem)
        await_row(s_send, t, ss_sem)
    await_all(moving.at[pl.ds(0, DEVICES - 1)], move_send.at[0])
    await_all(r_moving.at[pl.ds(0, DEVICES - 1)], move_send.at[1])


def per_device(
    grid_scalars, axial_speed, particles, cell_owner, cell_slot, mix_rate, partner,
    chem_input, chem_hidden, chem_output, react_slots, react_count, leave_slots, arrive_slots,
):
    vmem = pl.BlockSpec(memory_space=pltpu.VMEM)
    hbm = pl.BlockSpec(memory_space=pl.ANY)
    dma = pltpu.SemaphoreType.DMA
    messages = pltpu.VMEM((2, OWNERS, HALF, 128), F32)
    cells = pltpu.VMEM((DEVICES, 2, 14, 128), F32)
    short = pltpu.VMEM((DEVICES, 1, 128), F32)
    grid, out = pl.pallas_call(
        step_kernel,
        out_shape=(
            jax.ShapeDtypeStruct((4 * NS, 128), F32),
            jax.ShapeDtypeStruct((ROWS, CELLS), F32),
        ),
        in_specs=[vmem, vmem, hbm] + [vmem] * 11,
        out_specs=(vmem, hbm),
        scratch_shapes=[
            pltpu.VMEM((4, ROWS, 128), F32),
            pltpu.VMEM((2, ROWS, 128), F32),
            pltpu.VMEM((2, 2, 2, 56, 128), F32),
            pltpu.VMEM((2, 4, 2, 56, 128), F32),
            messages,
            messages,
            messages,
            messages,
            cells,
            cells,
            short,
            short,
            pltpu.VMEM((PLACES, CELLS), BF16),
            pltpu.VMEM((PLACES, CELLS), BF16),
            pltpu.VMEM((CELLS, CELLS), BF16),
            pltpu.VMEM((CELLS + LIST, CELLS), BF16),
            pltpu.VMEM((4, LIST, 128), F32),
            pltpu.VMEM((2, NP, CELLS), jnp.int32),
            pltpu.VMEM((CHAINS * WIDE, 64, LIST), F32),
            pltpu.VMEM((64, CELLS), F32),
            pltpu.VMEM((2, 64, 128), F32),
            pltpu.VMEM((64, LIST), F32),
            pltpu.VMEM((ROWS, CELLS), F32),
            pltpu.VMEM((128, 256), F32),
            pltpu.VMEM((64, 256), F32),
            dma((4,)),
            dma((ROWS // SPAN,)),
            dma((2, 4)),
            dma((2, 4)),
            dma((2,)),
            dma((2,)),
            dma((2,)),
            dma((2,)),
            dma((2,)),
            dma((2,)),
        ],
        compiler_params=pltpu.CompilerParams(
            collective_id=0, has_side_effects=True, vmem_limit_bytes=VMEM_LIMIT
        ),
        name="step",
    )(
        grid_scalars.reshape(4 * NS, 128),
        axial_speed.reshape(4, 128),
        particles.reshape(ROWS, CELLS),
        cell_owner.reshape(4, 128),
        cell_slot.reshape(4, 128),
        mix_rate.reshape(1, CELLS),
        partner,
        chem_input.T,
        chem_hidden,
        chem_output,
        react_slots,
        react_count.reshape(1, 1),
        leave_slots,
        arrive_slots,
    )
    return grid.reshape(grid_scalars.shape), out.reshape(particles.shape)


def solution(mesh):
    placed = (
        P(None, "gx", "gy", None),
        P("gx", "gy", None),
        P(None, None, ("gx", "gy")),
        P("gx", "gy", None),
        P("gx", "gy", None),
        P(("gx", "gy")),
        P(None, ("gx", "gy")),
        P(),
        P(),
        P(),
        P(("gx", "gy"), None),
        P(("gx", "gy")),
        P(("gx", "gy"), None),
        P(("gx", "gy"), None),
    )
    return jax.shard_map(
        per_device,
        mesh=mesh,
        in_specs=placed,
        out_specs=(P(None, "gx", "gy", None), P(None, None, ("gx", "gy"))),
        check_vma=False,
    )
```

```python
import functools

import jax
import jax.numpy as jnp
from jax import lax
from jax.experimental import pallas as pl
from jax.experimental.pallas import tpu as pltpu
from jax.sharding import PartitionSpec as P

F32, BF16 = jnp.float32, jnp.bfloat16
MESH = pl.DeviceIdType.MESH

NS, NP, CELLS = 54, 32, 512
ROWS = NS * NP
OWNERS, GROUPS, DEVICES = 32, 4, 128
HALF = 16
PLACES = 2 * OWNERS * HALF
LIST = 256
SPAN = 432
STRIDE = 37
PACE = (7, 33, 60)
CHAINS, WIDE = 2, 4
LABEL = 54
VMEM_LIMIT = 56 * 1024 * 1024
NT = (((1,), (1,)), ((), ()))


def split(x):
    hi = x.astype(BF16)
    return hi, (x - hi.astype(F32)).astype(BF16)


def mat(a, b):
    return jnp.dot(a, b, preferred_element_type=F32)


def mat_nt(a, b):
    return lax.dot_general(a, b, NT, preferred_element_type=F32)


def silu(a):
    h = (0.5 * a).astype(BF16)
    return h + h * jnp.tanh(h)


def packed(picker, values):
    hi, lo = split(values)
    both = mat_nt(picker, jnp.concatenate([hi, lo], axis=0))
    both = both + pltpu.roll(both, 64, axis=1)
    lane = lax.broadcasted_iota(jnp.int32, (PLACES // 2, 128), 1)
    return jnp.where(lane < 64, both[: PLACES // 2], both[PLACES // 2 :])


def unpacked(message, placer):
    turned = message.T
    values = jnp.concatenate([turned[:64], turned[64:]], axis=1)
    hi, lo = split(values)
    both = mat(jnp.concatenate([hi, lo], axis=0), placer)
    return both[:64] + both[64:]


def step_kernel(
    grid_in, speed, parts_in, owner, slot, rate, partner, w_in, w_hid, w_out, listed, count, leave, arrive,
    grid_out, parts_out,
    state, guest, faces, halo, f_send, f_recv, s_send, s_recv, moving, moved, r_moving, r_moved,
    to_box, to_slot, order, final, turn, mates, feed, r_f, r_late, r_g, made, wi, wo,
    load_sem, store_sem, halo_send, halo_recv, fs_sem, fr_sem, ss_sem, sr_sem, move_send, move_recv,
):
    gx, gy = lax.axis_index("gx"), lax.axis_index("gy")
    me = gx * OWNERS + gy
    barrier = pltpu.get_barrier_semaphore()

    loads = [
        pltpu.make_async_copy(parts_in.at[:, pl.ds(128 * lb, 128)], state.at[lb], load_sem.at[lb]) for lb in range(4)
    ]
    for copy in loads:
        copy.start()

    def device(k):
        other = lax.rem(me + k, DEVICES)
        return other, {"gx": other // OWNERS, "gy": lax.rem(other, OWNERS)}

    def greet(k, carry):
        pl.semaphore_signal(barrier, inc=1, device_id=device(k)[1], device_id_type=MESH)
        return carry

    lax.fori_loop(1, DEVICES, greet, 0)

    for q in range(4):
        faces[0, q // 2, q % 2, 0:NS, :] = grid_in[pl.ds(q, NS, stride=4), :]
        faces[0, q // 2, q % 2, NS:56, :] = jnp.zeros((56 - NS, 128), F32)

    pl.semaphore_wait(barrier, DEVICES - 1)

    def halo_copies(t):
        ahead = [
            (faces.at[t, 1], {"gx": lax.rem(gx + 1, GROUPS)}),
            (faces.at[t, 0], {"gx": lax.rem(gx + GROUPS - 1, GROUPS)}),
            (faces.at[t, :, 1], {"gy": lax.rem(gy + 1, OWNERS)}),
            (faces.at[t, :, 0], {"gy": lax.rem(gy + OWNERS - 1, OWNERS)}),
        ]
        return [
            pltpu.make_async_remote_copy(
                src_ref=source,
                dst_ref=halo.at[t, i],
                send_sem=halo_send.at[t, i],
                recv_sem=halo_recv.at[t, i],
                device_id=device,
                device_id_type=MESH,
            )
            for i, (source, device) in enumerate(ahead)
        ]

    def exchange(out, into, t, send_sem, recv_sem):
        def send(k, carry):
            other = lax.rem(gy + k, OWNERS)
            pltpu.make_async_remote_copy(
                src_ref=out.at[t, other],
                dst_ref=into.at[t, gy],
                send_sem=send_sem.at[t],
                recv_sem=recv_sem.at[t],
                device_id={"gy": other},
                device_id_type=MESH,
            ).start()
            return carry

        lax.fori_loop(1, OWNERS, send, 0)
        into[t, gy] = out[t, gy]

    def exchange_all(out, into, i, first=1, last=DEVICES):
        def send(k, carry):
            other, where = device(lax.rem(k * STRIDE, DEVICES))
            pltpu.make_async_remote_copy(
                src_ref=out.at[other],
                dst_ref=into.at[me],
                send_sem=move_send.at[i],
                recv_sem=move_recv.at[i],
                device_id=where,
                device_id_type=MESH,
            ).start()
            return carry

        lax.fori_loop(first, last, send, 0)
        if first == 1:
            into[me] = out[me]

    def await_all(part, sem):
        pltpu.make_async_copy(part, part, sem).wait()

    def await_row(buf, t, sem):
        await_all(buf.at[t, pl.ds(0, OWNERS - 1)], sem.at[t])

    halos = [halo_copies(t) for t in range(2)]
    for copy in halos[0]:
        copy.start()

    def iota(shape, dim):
        return lax.broadcasted_iota(jnp.int32, shape, dim)

    owner_row = jnp.concatenate([owner[q : q + 1, :] for q in range(4)], axis=1)
    label_row = jnp.concatenate([slot[q : q + 1, :] for q in range(4)], axis=1).astype(F32) + 1.0
    mine = (iota((OWNERS, CELLS), 0) == owner_row).astype(F32)
    before = (iota((CELLS, CELLS), 0) < iota((CELLS, CELLS), 1)).astype(F32)
    ahead = mat(mine.astype(BF16), before.astype(BF16))
    rank = jnp.sum(mine * ahead, axis=0, keepdims=True)
    place = owner_row.astype(F32) * HALF + rank + jnp.where(rank >= HALF, float(PLACES // 2 - HALF), 0.0)
    place = place.astype(jnp.int32)
    to_box[...] = (iota((PLACES, CELLS), 0) == place).astype(F32).astype(BF16)
    picks = (iota((CELLS, LIST), 0) == listed[...]).astype(F32)
    others = 1.0 - mat(picks.astype(BF16), jnp.ones((LIST, 128), BF16))
    later = (iota((CELLS, CELLS), 1) < iota((CELLS, CELLS), 0)).astype(F32)
    column = mat(later.astype(BF16), others.astype(BF16))
    column = jnp.where(others > 0.5, column, -1.0)[:, 0:1]
    rest = (column == iota((CELLS, LIST), 1).astype(F32)).astype(F32)
    chosen = jnp.concatenate([picks, rest], axis=1)
    order[...] = chosen.astype(BF16)
    live_row = (iota((1, LIST), 1) < count[...]).astype(F32)
    wi[...] = jnp.zeros_like(wi)
    wi[0:NS, :] = w_in[...].astype(F32)
    wo[...] = jnp.zeros_like(wo)
    wo[0:NS, :] = w_out[...].astype(F32)
    feed[...] = jnp.zeros_like(feed)
    weights_in = wi[...].T[:, 0:64].astype(BF16)
    weights_out = wo[...].astype(BF16)
    mates[0] = partner[...]

    def mix(t, keep_row):
        for lb in range(4):
            cols = slice(128 * lb, 128 * lb + 128)
            index = [mates[t, 8 * o : 8 * o + 8, cols] & 7 for o in range(4)]
            group = [mates[t, 8 * o : 8 * o + 8, cols] >> 3 for o in range(4)]
            late = t == 1 and lb >= 2

            def body(s, carry):
                base = pl.multiple_of(s * NP, NP)
                tiles = [state[lb, pl.ds(base + 8 * g, 8), :] for g in range(4)]
                for o in range(4):
                    mate = jnp.take_along_axis(tiles[0], index[o], axis=0, mode="promise_in_bounds")
                    for g in range(1, 4):
                        other = jnp.take_along_axis(tiles[g], index[o], axis=0, mode="promise_in_bounds")
                        mate = jnp.where(group[o] == g, other, mate)
                    mixed = 0.6 * tiles[o] + 0.4 * mate
                    if late:
                        mixed = mixed * keep_row[:, cols] + r_late[lb - 2, pl.ds(s, 1), :]
                    state[lb, pl.ds(base + 8 * o, 8), :] = mixed
                return carry

            lax.fori_loop(0, NS, body, 0, unroll=2)

    def rows_of(ref, blocks, start, size):
        return jnp.concatenate([ref[lb, start : start + size, :] for lb in range(blocks)], axis=1)

    def permute():
        for k in range(ROWS // SPAN):
            hi, lo = split(rows_of(state, 4, SPAN * k, SPAN))
            turned = mat(hi, order[...]) + mat(lo, order[...])
            for lb in range(4):
                state[lb, SPAN * k : SPAN * k + SPAN, :] = turned[:, 128 * lb : 128 * lb + 128]

    def transport(t):
        x_low = jnp.where(gx > 0, 1.0, 0.0).astype(F32)
        x_high = jnp.where(gx < GROUPS - 1, 1.0, 0.0).astype(F32)
        y_low = jnp.where(gy > 0, 1.0, 0.0).astype(F32)
        y_high = jnp.where(gy < OWNERS - 1, 1.0, 0.0).astype(F32)
        done = []
        for x in range(2):
            for y in range(2):
                center = faces[t, x, y]
                up = faces[t, 0, y] if x else halo[t, 0, y] * x_low
                down = halo[t, 1, y] * x_high if x else faces[t, 1, y]
                left = faces[t, x, 0] if y else halo[t, 2, x] * y_low
                right = halo[t, 3, x] * y_high if y else faces[t, x, 1]
                around = up + down + left + right
                around = around + pltpu.roll(center, 1, axis=1) + pltpu.roll(center, 127, axis=1)
                q = 2 * x + y
                done.append(center + 0.1 * (around - 6.0 * center) - speed[q : q + 1, :] * (center - up))
        return jnp.concatenate(done, axis=1)

    def chemistry(ref, keep, source, live):
        def body(g, total):
            for c in range(CHAINS):
                for i in range(WIDE):
                    p = (CHAINS * g + c) * WIDE + i
                    own = jnp.concatenate([ref[lb, pl.ds(p, NS, stride=NP), :] for lb in range(2)], axis=1)
                    feed[c * WIDE + i, 0:NS, :] = own * keep + source[0:NS, 0:LIST]
            columns = [
                jnp.concatenate(
                    [jnp.where(live > 0.5, feed[c * WIDE + i], 0.0).astype(BF16) for i in range(WIDE)], axis=1
                )
                for c in range(CHAINS)
            ]
            one = [silu(mat(weights_in, x)) for x in columns]
            two = [silu(mat(w_hid[...], x)) for x in one]
            change = [mat(weights_out, x).astype(BF16).astype(F32) for x in two]
            for c in range(CHAINS):
                for i in range(WIDE):
                    p = (CHAINS * g + c) * WIDE + i
                    part = jnp.where(live > 0.5, change[c][:, LIST * i : LIST * i + LIST], 0.0)
                    done = feed[c * WIDE + i] + part
                    for lb in range(2):
                        ref[lb, pl.ds(p, NS, stride=NP), :] = done[0:NS, 128 * lb : 128 * lb + 128]
                    total = total + part
            return total

        return lax.fori_loop(0, NP // (CHAINS * WIDE), body, jnp.zeros((64, LIST), F32))

    def through(values, matrix, product=mat):
        hi, lo = split(values)
        both = product(jnp.concatenate([hi, lo], axis=0), matrix)
        return both[: values.shape[0]] + both[values.shape[0] :]

    row = iota((64, CELLS), 0)
    for t in range(2):
        for copy in halos[t]:
            copy.wait_recv()
        grid = jnp.concatenate([transport(t), jnp.zeros((8, CELLS), F32)], axis=0)
        message = packed(to_box[...], jnp.where(row == LABEL, label_row, grid))
        for j in range(OWNERS):
            f_send[t, j] = message[HALF * j : HALF * j + HALF]
        exchange(f_send, f_recv, t, fs_sem, fr_sem)
        if t == 1:
            exchange_all(moving, moved, 0, PACE[1], PACE[2])
        if t == 0:
            for copy in loads:
                copy.wait()
            mix(0, None)
            permute()
            mates[1] = mat(partner[...].astype(F32).astype(BF16), order[...]).astype(jnp.int32)
            rate_row = through(jnp.broadcast_to(rate[...], (8, CELLS)), order[...])[0:1]
            keep_row = 1.0 - rate_row
            goes = (iota((CELLS, LIST), 0) == leave[...]).astype(F32)
            goes = mat(goes.T.astype(BF16), order[...])
            for lb in range(4):
                turn[lb] = goes[:, 128 * lb : 128 * lb + 128]
            halves = [
                jnp.concatenate([turn[lb, pl.ds(c, DEVICES, stride=2), :] for lb in range(4)], axis=1) for c in range(2)
            ]
            goes_halves = jnp.concatenate(halves, axis=0).astype(BF16)
            goes = goes.astype(BF16)
            lands = (iota((CELLS, LIST), 0) == arrive[...]).astype(F32)
            taken = mat_nt(jnp.ones((8, LIST), BF16), lands.astype(BF16))[0:1]
            lands = lands.T
            for lb in range(4):
                turn[lb] = lands[:, 128 * lb : 128 * lb + 128]
            final[0:CELLS, :] = jnp.where(taken > 0.5, 0.0, chosen.T).astype(BF16)
            for c in range(2):
                final[CELLS + DEVICES * c : CELLS + DEVICES * (c + 1), :] = jnp.concatenate(
                    [turn[lb, pl.ds(c, DEVICES, stride=2), :] for lb in range(4)], axis=1
                ).astype(BF16)
        await_row(f_recv, t, fr_sem)
        arrived = f_recv[t].reshape(PLACES // 2, 128)
        if t == 0:
            lane = iota((PLACES // 2, CELLS), 1).astype(F32) + 1.0
            for h in range(2):
                labels = arrived[:, 64 * h + LABEL : 64 * h + LABEL + 1]
                to_slot[h * PLACES // 2 : (h + 1) * PLACES // 2, :] = (labels == lane).astype(F32).astype(BF16)
        r_f[...] = through(unpacked(arrived, to_slot[...]), order[...]) * rate_row
        for lb in range(2):
            r_late[lb] = r_f[:, LIST + 128 * lb : LIST + 128 * lb + 128]
        if t == 1:
            hi, lo = split(r_f[...])
            both = mat_nt(goes_halves, jnp.concatenate([hi, lo], axis=0))
            both = both + pltpu.roll(both, 64, axis=1)
            r_moving[:, 0, :] = jnp.where(iota((DEVICES, 128), 1) < 64, both[:DEVICES], both[DEVICES:])
            exchange_all(r_moving, r_moved, 1)
            exchange_all(moving, moved, 0, PACE[2], DEVICES)
        total = chemistry(state, keep_row[:, 0:LIST], r_f, live_row)
        source = through(total * (1.0 / NP), order[:, 0:LIST], mat_nt)
        message = packed(to_slot[...], source)
        for j in range(OWNERS):
            s_send[t, j] = message[HALF * j : HALF * j + HALF]
        exchange(s_send, s_recv, t, ss_sem, sr_sem)
        if t == 0:
            mix(1, keep_row)
            for j in range(13):
                hi, lo = split(rows_of(state, 4, 128 * j, 128))
                value = mat_nt(goes, hi) + mat_nt(goes, lo)
                moving[:, :, j, :] = value.reshape(DEVICES, 2, 128)
            live_all = jnp.concatenate([live_row, jnp.zeros((1, LIST), F32)], axis=1)
            extra = jnp.where(row == 0, rate_row, jnp.where(row == 1, live_all, 0.0))
            hi, lo = split(jnp.concatenate([rows_of(state, 4, 1664, 64), extra], axis=0))
            value = mat_nt(goes, hi) + mat_nt(goes, lo)
            moving[:, :, 13, :] = value.reshape(DEVICES, 2, 128)
            exchange_all(moving, moved, 0, 1, PACE[0])
        else:
            await_all(moved.at[pl.ds(0, DEVICES - 1)], move_recv.at[0])
            await_all(r_moved.at[pl.ds(0, DEVICES - 1)], move_recv.at[1])
            metas = []
            for c in range(2):
                for j in range(14):
                    block = moved[:, c, j, :].T
                    size = min(128, ROWS - 128 * j)
                    guest[c, 128 * j : 128 * j + size, :] = block[0:size]
                metas.append(block[64:72])
            metas = jnp.concatenate(metas, axis=1)
            r_turned = r_moved[...].reshape(DEVICES, 128).T
            r_g[...] = jnp.concatenate([r_turned[0:64], r_turned[64:128]], axis=1)
            chemistry(guest, 1.0 - metas[0:1], r_g, metas[1:2])

            def relax(s, carry):
                base = pl.multiple_of(s * NP, NP)
                for lb in range(2, 4):
                    cols = slice(128 * lb, 128 * lb + 128)
                    span = pl.ds(base, NP)
                    state[lb, span, :] = state[lb, span, :] * keep_row[:, cols] + r_late[lb - 2, pl.ds(s, 1), :]
                return carry

            lax.fori_loop(0, NS, relax, 0)
            stores = [
                pltpu.make_async_copy(
                    made.at[pl.ds(SPAN * k, SPAN)], parts_out.at[pl.ds(SPAN * k, SPAN)], store_sem.at[k]
                )
                for k in range(ROWS // SPAN)
            ]
            for k in range(ROWS // SPAN):
                block = [rows_of(state, 4, SPAN * k, SPAN), rows_of(guest, 2, SPAN * k, SPAN)]
                hi, lo = split(jnp.concatenate(block, axis=1))
                made[SPAN * k : SPAN * k + SPAN, :] = mat(hi, final[...]) + mat(lo, final[...])
                stores[k].start()
        await_row(s_recv, t, sr_sem)
        grid = grid + unpacked(s_recv[t].reshape(PLACES // 2, 128), to_box[...])
        if t == 0:
            for q in range(4):
                faces[1, q // 2, q % 2] = grid[0:56, 128 * q : 128 * q + 128]
            for copy in halos[1]:
                copy.start()
            exchange_all(moving, moved, 0, PACE[0], PACE[1])
        else:
            for q in range(4):
                grid_out[pl.ds(q, NS, stride=4), :] = grid[0:NS, 128 * q : 128 * q + 128]
    for copy in stores:
        copy.wait()
    for t in range(2):
        for copy in halos[t]:
            copy.wait_send()
        await_row(f_send, t, fs_sem)
        await_row(s_send, t, ss_sem)
    await_all(moving.at[pl.ds(0, DEVICES - 1)], move_send.at[0])
    await_all(r_moving.at[pl.ds(0, DEVICES - 1)], move_send.at[1])


def per_device(
    grid_scalars, axial_speed, particles, cell_owner, cell_slot, mix_rate, partner,
    chem_input, chem_hidden, chem_output, react_slots, react_count, leave_slots, arrive_slots,
):
    vmem = pl.BlockSpec(memory_space=pltpu.VMEM)
    hbm = pl.BlockSpec(memory_space=pl.ANY)
    dma = pltpu.SemaphoreType.DMA
    messages = pltpu.VMEM((2, OWNERS, HALF, 128), F32)
    cells = pltpu.VMEM((DEVICES, 2, 14, 128), F32)
    short = pltpu.VMEM((DEVICES, 1, 128), F32)
    grid, out = pl.pallas_call(
        step_kernel,
        out_shape=(
            jax.ShapeDtypeStruct((4 * NS, 128), F32),
            jax.ShapeDtypeStruct((ROWS, CELLS), F32),
        ),
        in_specs=[vmem, vmem, hbm] + [vmem] * 11,
        out_specs=(vmem, hbm),
        scratch_shapes=[
            pltpu.VMEM((4, ROWS, 128), F32),
            pltpu.VMEM((2, ROWS, 128), F32),
            pltpu.VMEM((2, 2, 2, 56, 128), F32),
            pltpu.VMEM((2, 4, 2, 56, 128), F32),
            messages,
            messages,
            messages,
            messages,
            cells,
            cells,
            short,
            short,
            pltpu.VMEM((PLACES, CELLS), BF16),
            pltpu.VMEM((PLACES, CELLS), BF16),
            pltpu.VMEM((CELLS, CELLS), BF16),
            pltpu.VMEM((CELLS + LIST, CELLS), BF16),
            pltpu.VMEM((4, LIST, 128), F32),
            pltpu.VMEM((2, NP, CELLS), jnp.int32),
            pltpu.VMEM((CHAINS * WIDE, 64, LIST), F32),
            pltpu.VMEM((64, CELLS), F32),
            pltpu.VMEM((2, 64, 128), F32),
            pltpu.VMEM((64, LIST), F32),
            pltpu.VMEM((ROWS, CELLS), F32),
            pltpu.VMEM((128, 256), F32),
            pltpu.VMEM((64, 256), F32),
            dma((4,)),
            dma((ROWS // SPAN,)),
            dma((2, 4)),
            dma((2, 4)),
            dma((2,)),
            dma((2,)),
            dma((2,)),
            dma((2,)),
            dma((2,)),
            dma((2,)),
        ],
        compiler_params=pltpu.CompilerParams(
            collective_id=0, has_side_effects=True, vmem_limit_bytes=VMEM_LIMIT
        ),
        name="step",
    )(
        grid_scalars.reshape(4 * NS, 128),
        axial_speed.reshape(4, 128),
        particles.reshape(ROWS, CELLS),
        cell_owner.reshape(4, 128),
        cell_slot.reshape(4, 128),
        mix_rate.reshape(1, CELLS),
        partner,
        chem_input.T,
        chem_hidden,
        chem_output,
        react_slots,
        react_count.reshape(1, 1),
        leave_slots,
        arrive_slots,
    )
    return grid.reshape(grid_scalars.shape), out.reshape(particles.shape)


def solution(mesh):
    placed = (
        P(None, "gx", "gy", None),
        P("gx", "gy", None),
        P(None, None, ("gx", "gy")),
        P("gx", "gy", None),
        P("gx", "gy", None),
        P(("gx", "gy")),
        P(None, ("gx", "gy")),
        P(),
        P(),
        P(),
        P(("gx", "gy"), None),
        P(("gx", "gy")),
        P(("gx", "gy"), None),
        P(("gx", "gy"), None),
    )
    return jax.shard_map(
        per_device,
        mesh=mesh,
        in_specs=placed,
        out_specs=(P(None, "gx", "gy", None), P(None, None, ("gx", "gy"))),
        check_vma=False,
    )
```

```python
import functools

import jax
import jax.numpy as jnp
from jax import lax
from jax.experimental import pallas as pl
from jax.experimental.pallas import tpu as pltpu
from jax.sharding import PartitionSpec as P

F32, BF16 = jnp.float32, jnp.bfloat16
MESH = pl.DeviceIdType.MESH

NS, NP, CELLS = 54, 32, 512
ROWS = NS * NP
OWNERS, GROUPS, DEVICES = 32, 4, 128
HALF = 16
PLACES = 2 * OWNERS * HALF
LIST = 256
SPAN = 432
STRIDE = 37
PACE = (30, 60)
CHAINS, WIDE = 2, 4
LABEL = 54
VMEM_LIMIT = 56 * 1024 * 1024
NT = (((1,), (1,)), ((), ()))


def split(x):
    hi = x.astype(BF16)
    return hi, (x - hi.astype(F32)).astype(BF16)


def mat(a, b):
    return jnp.dot(a, b, preferred_element_type=F32)


def mat_nt(a, b):
    return lax.dot_general(a, b, NT, preferred_element_type=F32)


def silu(a):
    return (a + a * jnp.tanh(a)).astype(BF16)


def packed(picker, values):
    hi, lo = split(values)
    both = mat_nt(picker, jnp.concatenate([hi, lo], axis=0))
    both = both + pltpu.roll(both, 64, axis=1)
    lane = lax.broadcasted_iota(jnp.int32, (PLACES // 2, 128), 1)
    return jnp.where(lane < 64, both[: PLACES // 2], both[PLACES // 2 :])


def unpacked(message, placer):
    turned = message.T
    values = jnp.concatenate([turned[:64], turned[64:]], axis=1)
    hi, lo = split(values)
    both = mat(jnp.concatenate([hi, lo], axis=0), placer)
    return both[:64] + both[64:]


def step_kernel(
    grid_in, speed, parts_in, owner, slot, rate, partner, w_in, w_hid, w_out, listed, count, leave, arrive,
    grid_out, parts_out,
    state, guest, faces, halo, f_send, f_recv, s_send, s_recv, moving, moved, r_moving, r_moved,
    to_box, to_slot, order, final, turn, goes_halves, mates, feed, r_f, r_late, r_g, made, wi, wo,
    load_sem, store_sem, halo_send, halo_recv, fs_sem, fr_sem, ss_sem, sr_sem, move_send, move_recv,
):
    gx, gy = lax.axis_index("gx"), lax.axis_index("gy")
    me = gx * OWNERS + gy
    barrier = pltpu.get_barrier_semaphore()

    loads = [
        pltpu.make_async_copy(parts_in.at[:, pl.ds(128 * lb, 128)], state.at[lb], load_sem.at[lb]) for lb in range(4)
    ]
    for copy in loads:
        copy.start()

    def device(k):
        other = lax.rem(me + k, DEVICES)
        return other, {"gx": other // OWNERS, "gy": lax.rem(other, OWNERS)}

    def greet(k, carry):
        pl.semaphore_signal(barrier, inc=1, device_id=device(k)[1], device_id_type=MESH)
        return carry

    lax.fori_loop(1, DEVICES, greet, 0)

    for q in range(4):
        faces[0, q // 2, q % 2, 0:NS, :] = grid_in[pl.ds(q, NS, stride=4), :]
        faces[0, q // 2, q % 2, NS:56, :] = jnp.zeros((56 - NS, 128), F32)

    pl.semaphore_wait(barrier, DEVICES - 1)

    def halo_copies(t):
        ahead = [
            (faces.at[t, 1], {"gx": lax.rem(gx + 1, GROUPS)}),
            (faces.at[t, 0], {"gx": lax.rem(gx + GROUPS - 1, GROUPS)}),
            (faces.at[t, :, 1], {"gy": lax.rem(gy + 1, OWNERS)}),
            (faces.at[t, :, 0], {"gy": lax.rem(gy + OWNERS - 1, OWNERS)}),
        ]
        return [
            pltpu.make_async_remote_copy(
                src_ref=source,
                dst_ref=halo.at[t, i],
                send_sem=halo_send.at[t, i],
                recv_sem=halo_recv.at[t, i],
                device_id=device,
                device_id_type=MESH,
            )
            for i, (source, device) in enumerate(ahead)
        ]

    def exchange(out, into, t, send_sem, recv_sem):
        def send(k, carry):
            other = lax.rem(gy + k, OWNERS)
            pltpu.make_async_remote_copy(
                src_ref=out.at[t, other],
                dst_ref=into.at[t, gy],
                send_sem=send_sem.at[t],
                recv_sem=recv_sem.at[t],
                device_id={"gy": other},
                device_id_type=MESH,
            ).start()
            return carry

        lax.fori_loop(1, OWNERS, send, 0)
        into[t, gy] = out[t, gy]

    def exchange_all(out, into, c, i, first=1, last=DEVICES):
        def send(k, carry):
            other, where = device(lax.rem(k * STRIDE, DEVICES))
            pltpu.make_async_remote_copy(
                src_ref=out.at[c, other],
                dst_ref=into.at[c, me],
                send_sem=move_send.at[i],
                recv_sem=move_recv.at[i],
                device_id=where,
                device_id_type=MESH,
            ).start()
            return carry

        lax.fori_loop(first, last, send, 0)
        if first == 1:
            into[c, me] = out[c, me]

    def await_cells(buf, c, sem):
        await_all(buf.at[c, pl.ds(0, DEVICES - 1)], sem)

    def await_all(part, sem):
        pltpu.make_async_copy(part, part, sem).wait()

    def await_row(buf, t, sem):
        await_all(buf.at[t, pl.ds(0, OWNERS - 1)], sem.at[t])

    halos = [halo_copies(t) for t in range(2)]
    for copy in halos[0]:
        copy.start()

    def iota(shape, dim):
        return lax.broadcasted_iota(jnp.int32, shape, dim)

    owner_row = jnp.concatenate([owner[q : q + 1, :] for q in range(4)], axis=1)
    label_row = jnp.concatenate([slot[q : q + 1, :] for q in range(4)], axis=1).astype(F32) + 1.0
    mine = (iota((OWNERS, CELLS), 0) == owner_row).astype(F32)
    before = (iota((CELLS, CELLS), 0) < iota((CELLS, CELLS), 1)).astype(F32)
    ahead = mat(mine.astype(BF16), before.astype(BF16))
    rank = jnp.sum(mine * ahead, axis=0, keepdims=True)
    place = owner_row.astype(F32) * HALF + rank + jnp.where(rank >= HALF, float(PLACES // 2 - HALF), 0.0)
    place = place.astype(jnp.int32)
    to_box[...] = (iota((PLACES, CELLS), 0) == place).astype(F32).astype(BF16)
    picks = (iota((CELLS, LIST), 0) == listed[...]).astype(F32)
    others = 1.0 - mat(picks.astype(BF16), jnp.ones((LIST, 128), BF16))
    later = (iota((CELLS, CELLS), 1) < iota((CELLS, CELLS), 0)).astype(F32)
    column = mat(later.astype(BF16), others.astype(BF16))
    column = jnp.where(others > 0.5, column, -1.0)[:, 0:1]
    rest = (column == iota((CELLS, LIST), 1).astype(F32)).astype(F32)
    chosen = jnp.concatenate([picks, rest], axis=1)
    order[...] = chosen.astype(BF16)
    live_row = (iota((1, LIST), 1) < count[...]).astype(F32)
    wi[...] = jnp.zeros_like(wi)
    wi[0:NS, :] = w_in[...].astype(F32)
    wo[...] = jnp.zeros_like(wo)
    wo[0:NS, :] = w_out[...].astype(F32)
    feed[...] = jnp.zeros_like(feed)
    weights_in = (0.5 * wi[...].T[:, 0:64]).astype(BF16)
    weights_hid = (0.5 * w_hid[...].astype(F32)).astype(BF16)
    weights_out = wo[...].astype(BF16)

    def mix(ref, lb, mate_of, keep=None, late=None):
        index = [mate_of[8 * o : 8 * o + 8] & 7 for o in range(4)]
        group = [mate_of[8 * o : 8 * o + 8] >> 3 for o in range(4)]

        def body(s, carry):
            base = pl.multiple_of(s * NP, NP)
            tiles = [ref[lb, pl.ds(base + 8 * g, 8), :] for g in range(4)]
            for o in range(4):
                mate = jnp.take_along_axis(tiles[0], index[o], axis=0, mode="promise_in_bounds")
                for g in range(1, 4):
                    other = jnp.take_along_axis(tiles[g], index[o], axis=0, mode="promise_in_bounds")
                    mate = jnp.where(group[o] == g, other, mate)
                mixed = 0.6 * tiles[o] + 0.4 * mate
                if keep is not None:
                    mixed = mixed * keep + r_late[late, pl.ds(s, 1), :]
                ref[lb, pl.ds(base + 8 * o, 8), :] = mixed
            return carry

        lax.fori_loop(0, NS, body, 0, unroll=2)

    def pack_cells(c, goes_c, extra):
        for j in range(14):
            if j < 13:
                value = rows_of(state, 4, 128 * j, 128)
            else:
                value = jnp.concatenate([rows_of(state, 4, 1664, 64), extra], axis=0)
            hi, lo = split(value)
            moving[c, :, j, :] = mat_nt(goes_c, hi) + mat_nt(goes_c, lo)

    def unpack_cells(c):
        for j in range(14):
            block = moved[c, :, j, :].T
            size = min(128, ROWS - 128 * j)
            guest[c, 128 * j : 128 * j + size, :] = block[0:size]
        return block[64:72], block[96:128]

    def rows_of(ref, blocks, start, size):
        return jnp.concatenate([ref[lb, start : start + size, :] for lb in range(blocks)], axis=1)

    def permute():
        for k in range(ROWS // SPAN):
            hi, lo = split(rows_of(state, 4, SPAN * k, SPAN))
            turned = mat(hi, order[...]) + mat(lo, order[...])
            for lb in range(4):
                state[lb, SPAN * k : SPAN * k + SPAN, :] = turned[:, 128 * lb : 128 * lb + 128]

    def transport(t):
        x_low = jnp.where(gx > 0, 1.0, 0.0).astype(F32)
        x_high = jnp.where(gx < GROUPS - 1, 1.0, 0.0).astype(F32)
        y_low = jnp.where(gy > 0, 1.0, 0.0).astype(F32)
        y_high = jnp.where(gy < OWNERS - 1, 1.0, 0.0).astype(F32)
        done = []
        for x in range(2):
            for y in range(2):
                center = faces[t, x, y]
                up = faces[t, 0, y] if x else halo[t, 0, y] * x_low
                down = halo[t, 1, y] * x_high if x else faces[t, 1, y]
                left = faces[t, x, 0] if y else halo[t, 2, x] * y_low
                right = halo[t, 3, x] * y_high if y else faces[t, x, 1]
                around = up + down + left + right
                around = around + pltpu.roll(center, 1, axis=1) + pltpu.roll(center, 127, axis=1)
                q = 2 * x + y
                done.append(center + 0.1 * (around - 6.0 * center) - speed[q : q + 1, :] * (center - up))
        return jnp.concatenate(done, axis=1)

    def chemistry(ref, blocks, keep, source, live):
        width = 128 * blocks
        wide = WIDE * 2 // blocks
        chains = range(CHAINS)

        def body(g, total):
            for c in chains:
                for i in range(wide):
                    p = (CHAINS * g + c) * wide + i
                    own = jnp.concatenate([ref[lb, pl.ds(p, NS, stride=NP), :] for lb in range(blocks)], axis=1)
                    feed[c * wide + i, 0:NS, 0:width] = own * keep + source[0:NS, 0:width]
            columns = [
                jnp.concatenate(
                    [
                        jnp.where(live > 0.5, feed[c * wide + i, :, 0:width], 0.0).astype(BF16)
                        for i in range(wide)
                    ],
                    axis=1,
                )
                for c in chains
            ]
            one = [silu(mat(weights_in, x)) for x in columns]
            two = [silu(mat(weights_hid, x)) for x in one]
            change = [mat(weights_out, x).astype(BF16).astype(F32) for x in two]
            for c in chains:
                for i in range(wide):
                    p = (CHAINS * g + c) * wide + i
                    part = jnp.where(live > 0.5, change[c][:, width * i : width * i + width], 0.0)
                    done = feed[c * wide + i, :, 0:width] + part
                    for lb in range(blocks):
                        ref[lb, pl.ds(p, NS, stride=NP), :] = done[0:NS, 128 * lb : 128 * lb + 128]
                    total = total + part
            return total

        return lax.fori_loop(0, NP // (CHAINS * wide), body, jnp.zeros((64, width), F32))

    def through(values, matrix, product=mat):
        hi, lo = split(values)
        both = product(jnp.concatenate([hi, lo], axis=0), matrix)
        return both[: values.shape[0]] + both[values.shape[0] :]

    for copy in loads[0:2]:
        copy.wait()
    for lb in range(2):
        mix(state, lb, partner[:, 128 * lb : 128 * lb + 128])
    row = iota((64, CELLS), 0)
    for t in range(2):
        if t == 1:
            await_cells(moved, 0, move_recv.at[0])
            await_cells(r_moved, 0, move_recv.at[2])
            meta, mate_of = unpack_cells(0)
            r_g[:, 0:128] = r_moved[0].reshape(DEVICES, 128).T[0:64]
            guest_keep, guest_live = 1.0 - meta[0:1], meta[1:2]
            guest_mates = mate_of.astype(jnp.int32)
            chemistry(guest, 1, guest_keep, r_g, guest_live)
        for copy in halos[t]:
            copy.wait_recv()
        grid = jnp.concatenate([transport(t), jnp.zeros((8, CELLS), F32)], axis=0)
        message = packed(to_box[...], jnp.where(row == LABEL, label_row, grid))
        for j in range(OWNERS):
            f_send[t, j] = message[HALF * j : HALF * j + HALF]
        exchange(f_send, f_recv, t, fs_sem, fr_sem)
        if t == 0:
            for copy in loads[2:4]:
                copy.wait()
            for lb in range(2, 4):
                mix(state, lb, partner[:, 128 * lb : 128 * lb + 128])
            permute()
            mates_now = mat(partner[...].astype(F32).astype(BF16), order[...])
            rate_row = through(jnp.broadcast_to(rate[...], (8, CELLS)), order[...])[0:1]
            keep_row = 1.0 - rate_row
            goes = (iota((CELLS, LIST), 0) == leave[...]).astype(F32)
            goes = mat(goes.T.astype(BF16), order[...])
            for lb in range(4):
                turn[lb] = goes[:, 128 * lb : 128 * lb + 128]
            for c in range(2):
                goes_halves[DEVICES * c : DEVICES * c + DEVICES, :] = jnp.concatenate(
                    [turn[lb, pl.ds(c, DEVICES, stride=2), :] for lb in range(4)], axis=1
                ).astype(BF16)
            live_all = jnp.concatenate([live_row, jnp.zeros((1, LIST), F32)], axis=1)
            extra = jnp.where(row == 0, rate_row, jnp.where(row == 1, live_all, 0.0))
            extra = jnp.concatenate([extra[0:32], mates_now], axis=0)
            mates[...] = extra
            pack_cells(0, goes_halves[0:DEVICES], extra)
            exchange_all(moving, moved, 0, 0)
        else:
            exchange_all(moving, moved, 1, 1, PACE[0], PACE[1])
            mix(guest, 0, guest_mates)
            lands = (iota((CELLS, LIST), 0) == arrive[...]).astype(F32)
            taken = mat_nt(jnp.ones((8, LIST), BF16), lands.astype(BF16))[0:1]
            lands = lands.T
            for lb in range(4):
                turn[lb] = lands[:, 128 * lb : 128 * lb + 128]
            final[0:CELLS, :] = jnp.where(taken > 0.5, 0.0, order[...].astype(F32).T).astype(BF16)
            for c in range(2):
                final[CELLS + DEVICES * c : CELLS + DEVICES * (c + 1), :] = jnp.concatenate(
                    [turn[lb, pl.ds(c, DEVICES, stride=2), :] for lb in range(4)], axis=1
                ).astype(BF16)
        await_row(f_recv, t, fr_sem)
        arrived = f_recv[t].reshape(PLACES // 2, 128)
        if t == 0:
            lane = iota((PLACES // 2, CELLS), 1).astype(F32) + 1.0
            for h in range(2):
                labels = arrived[:, 64 * h + LABEL : 64 * h + LABEL + 1]
                to_slot[h * PLACES // 2 : (h + 1) * PLACES // 2, :] = (labels == lane).astype(F32).astype(BF16)
        r_f[...] = through(unpacked(arrived, to_slot[...]), order[...]) * rate_row
        for lb in range(2):
            r_late[lb] = r_f[:, LIST + 128 * lb : LIST + 128 * lb + 128]
        hi, lo = split(r_f[...])
        both = mat_nt(goes_halves[...], jnp.concatenate([hi, lo], axis=0))
        both = both + pltpu.roll(both, 64, axis=1)
        r_moving[t, :, 0, :] = jnp.where(iota((DEVICES, 128), 1) < 64, both[:DEVICES], both[DEVICES:])
        exchange_all(r_moving, r_moved, t, 2 + t)
        if t == 1:
            exchange_all(moving, moved, 1, 1, PACE[1], DEVICES)
        total = chemistry(state, 2, keep_row[:, 0:LIST], r_f, live_row)
        source = through(total * (1.0 / NP), order[:, 0:LIST], mat_nt)
        message = packed(to_slot[...], source)
        for j in range(OWNERS):
            s_send[t, j] = message[HALF * j : HALF * j + HALF]
        exchange(s_send, s_recv, t, ss_sem, sr_sem)
        if t == 0:
            for lb in range(4):
                cols = slice(128 * lb, 128 * lb + 128)
                mate_of = mates[32:64, cols].astype(jnp.int32)
                if lb < 2:
                    mix(state, lb, mate_of)
                else:
                    mix(state, lb, mate_of, keep_row[:, cols], lb - 2)
            pack_cells(1, goes_halves[DEVICES:], mates[...])
        else:
            await_cells(moved, 1, move_recv.at[1])
            await_cells(r_moved, 1, move_recv.at[3])
            late_meta, _ = unpack_cells(1)
            r_turned = r_moved[1].reshape(DEVICES, 128).T
            r_g[...] = jnp.concatenate([r_turned[0:64], r_turned[64:128]], axis=1)
            guest_keep = jnp.concatenate([guest_keep, 1.0 - late_meta[0:1]], axis=1)
            guest_live = jnp.concatenate([guest_live, late_meta[1:2]], axis=1)
            chemistry(guest, 2, guest_keep, r_g, guest_live)

            def relax(s, carry):
                base = pl.multiple_of(s * NP, NP)
                for lb in range(2, 4):
                    cols = slice(128 * lb, 128 * lb + 128)
                    span = pl.ds(base, NP)
                    state[lb, span, :] = state[lb, span, :] * keep_row[:, cols] + r_late[lb - 2, pl.ds(s, 1), :]
                return carry

            lax.fori_loop(0, NS, relax, 0)
            stores = [
                pltpu.make_async_copy(
                    made.at[pl.ds(SPAN * k, SPAN)], parts_out.at[pl.ds(SPAN * k, SPAN)], store_sem.at[k]
                )
                for k in range(ROWS // SPAN)
            ]
            for k in range(ROWS // SPAN):
                block = [rows_of(state, 4, SPAN * k, SPAN), rows_of(guest, 2, SPAN * k, SPAN)]
                hi, lo = split(jnp.concatenate(block, axis=1))
                made[SPAN * k : SPAN * k + SPAN, :] = mat(hi, final[...]) + mat(lo, final[...])
                stores[k].start()
        await_row(s_recv, t, sr_sem)
        grid = grid + unpacked(s_recv[t].reshape(PLACES // 2, 128), to_box[...])
        if t == 0:
            for q in range(4):
                faces[1, q // 2, q % 2] = grid[0:56, 128 * q : 128 * q + 128]
            for copy in halos[1]:
                copy.start()
            exchange_all(moving, moved, 1, 1, 1, PACE[0])
        else:
            for q in range(4):
                grid_out[pl.ds(q, NS, stride=4), :] = grid[0:NS, 128 * q : 128 * q + 128]
    for copy in stores:
        copy.wait()
    for t in range(2):
        for copy in halos[t]:
            copy.wait_send()
        await_row(f_send, t, fs_sem)
        await_row(s_send, t, ss_sem)
        await_cells(moving, t, move_send.at[t])
        await_cells(r_moving, t, move_send.at[2 + t])


def per_device(
    grid_scalars, axial_speed, particles, cell_owner, cell_slot, mix_rate, partner,
    chem_input, chem_hidden, chem_output, react_slots, react_count, leave_slots, arrive_slots,
):
    vmem = pl.BlockSpec(memory_space=pltpu.VMEM)
    hbm = pl.BlockSpec(memory_space=pl.ANY)
    dma = pltpu.SemaphoreType.DMA
    messages = pltpu.VMEM((2, OWNERS, HALF, 128), F32)
    cells = pltpu.VMEM((2, DEVICES, 14, 128), F32)
    short = pltpu.VMEM((2, DEVICES, 1, 128), F32)
    grid, out = pl.pallas_call(
        step_kernel,
        out_shape=(
            jax.ShapeDtypeStruct((4 * NS, 128), F32),
            jax.ShapeDtypeStruct((ROWS, CELLS), F32),
        ),
        in_specs=[vmem, vmem, hbm] + [vmem] * 11,
        out_specs=(vmem, hbm),
        scratch_shapes=[
            pltpu.VMEM((4, ROWS, 128), F32),
            pltpu.VMEM((2, ROWS, 128), F32),
            pltpu.VMEM((2, 2, 2, 56, 128), F32),
            pltpu.VMEM((2, 4, 2, 56, 128), F32),
            messages,
            messages,
            messages,
            messages,
            cells,
            cells,
            short,
            short,
            pltpu.VMEM((PLACES, CELLS), BF16),
            pltpu.VMEM((PLACES, CELLS), BF16),
            pltpu.VMEM((CELLS, CELLS), BF16),
            pltpu.VMEM((CELLS + LIST, CELLS), BF16),
            pltpu.VMEM((4, LIST, 128), F32),
            pltpu.VMEM((LIST, CELLS), BF16),
            pltpu.VMEM((64, CELLS), F32),
            pltpu.VMEM((CHAINS * WIDE * 2, 64, LIST), F32),
            pltpu.VMEM((64, CELLS), F32),
            pltpu.VMEM((2, 64, 128), F32),
            pltpu.VMEM((64, LIST), F32),
            pltpu.VMEM((ROWS, CELLS), F32),
            pltpu.VMEM((128, 256), F32),
            pltpu.VMEM((64, 256), F32),
            dma((4,)),
            dma((ROWS // SPAN,)),
            dma((2, 4)),
            dma((2, 4)),
            dma((2,)),
            dma((2,)),
            dma((2,)),
            dma((2,)),
            dma((4,)),
            dma((4,)),
        ],
        compiler_params=pltpu.CompilerParams(
            collective_id=0, has_side_effects=True, vmem_limit_bytes=VMEM_LIMIT
        ),
        name="step",
    )(
        grid_scalars.reshape(4 * NS, 128),
        axial_speed.reshape(4, 128),
        particles.reshape(ROWS, CELLS),
        cell_owner.reshape(4, 128),
        cell_slot.reshape(4, 128),
        mix_rate.reshape(1, CELLS),
        partner,
        chem_input.T,
        chem_hidden,
        chem_output,
        react_slots,
        react_count.reshape(1, 1),
        leave_slots,
        arrive_slots,
    )
    return grid.reshape(grid_scalars.shape), out.reshape(particles.shape)


def solution(mesh):
    placed = (
        P(None, "gx", "gy", None),
        P("gx", "gy", None),
        P(None, None, ("gx", "gy")),
        P("gx", "gy", None),
        P("gx", "gy", None),
        P(("gx", "gy")),
        P(None, ("gx", "gy")),
        P(),
        P(),
        P(),
        P(("gx", "gy"), None),
        P(("gx", "gy")),
        P(("gx", "gy"), None),
        P(("gx", "gy"), None),
    )
    return jax.shard_map(
        per_device,
        mesh=mesh,
        in_specs=placed,
        out_specs=(P(None, "gx", "gy", None), P(None, None, ("gx", "gy"))),
        check_vma=False,
    )
```

```python
import functools

import jax
import jax.numpy as jnp
from jax import lax
from jax.experimental import pallas as pl
from jax.experimental.pallas import tpu as pltpu
from jax.sharding import PartitionSpec as P

F32, BF16 = jnp.float32, jnp.bfloat16
MESH = pl.DeviceIdType.MESH

NS, NP, CELLS = 54, 32, 512
ROWS = NS * NP
OWNERS, GROUPS, DEVICES = 32, 4, 128
HALF = 16
PLACES = 2 * OWNERS * HALF
LIST = 256
SPAN = 432
STRIDE = 37
EARLY = 90
PACE = (30, 60)
CHAINS, WIDE = 2, 4
LABEL = 54
VMEM_LIMIT = 56 * 1024 * 1024
NT = (((1,), (1,)), ((), ()))


def split(x):
    hi = x.astype(BF16)
    return hi, (x - hi.astype(F32)).astype(BF16)


def mat(a, b):
    return jnp.dot(a, b, preferred_element_type=F32)


def mat_nt(a, b):
    return lax.dot_general(a, b, NT, preferred_element_type=F32)


def silu(a):
    return (a + a * jnp.tanh(a)).astype(BF16)


def packed(picker, values):
    hi, lo = split(values)
    both = mat_nt(picker, jnp.concatenate([hi, lo], axis=0))
    both = both + pltpu.roll(both, 64, axis=1)
    lane = lax.broadcasted_iota(jnp.int32, (PLACES // 2, 128), 1)
    return jnp.where(lane < 64, both[: PLACES // 2], both[PLACES // 2 :])


def unpacked(message, placer):
    turned = message.T
    values = jnp.concatenate([turned[:64], turned[64:]], axis=1)
    hi, lo = split(values)
    both = mat(jnp.concatenate([hi, lo], axis=0), placer)
    return both[:64] + both[64:]


def step_kernel(
    grid_in, speed, parts_in, owner, slot, rate, partner, w_in, w_hid, w_out, listed, count, leave, arrive,
    grid_out, parts_out,
    state, guest, faces, halo, f_send, f_recv, s_send, s_recv, moving, moved, r_moving, r_moved,
    to_box, to_slot, order, final, turn, goes_halves, mates, feed, r_f, r_late, r_g, made, wi, wo,
    load_sem, store_sem, halo_send, halo_recv, fs_sem, fr_sem, ss_sem, sr_sem, move_send, move_recv,
):
    gx, gy = lax.axis_index("gx"), lax.axis_index("gy")
    me = gx * OWNERS + gy
    barrier = pltpu.get_barrier_semaphore()

    loads = [
        pltpu.make_async_copy(parts_in.at[:, pl.ds(128 * lb, 128)], state.at[lb], load_sem.at[lb]) for lb in range(4)
    ]
    for copy in loads:
        copy.start()

    def device(k):
        other = lax.rem(me + k, DEVICES)
        return other, {"gx": other // OWNERS, "gy": lax.rem(other, OWNERS)}

    def greet(k, carry):
        pl.semaphore_signal(barrier, inc=1, device_id=device(k)[1], device_id_type=MESH)
        return carry

    lax.fori_loop(1, DEVICES, greet, 0)

    for q in range(4):
        faces[0, q // 2, q % 2, 0:NS, :] = grid_in[pl.ds(q, NS, stride=4), :]
        faces[0, q // 2, q % 2, NS:56, :] = jnp.zeros((56 - NS, 128), F32)

    pl.semaphore_wait(barrier, DEVICES - 1)

    def halo_copies(t):
        ahead = [
            (faces.at[t, 1], {"gx": lax.rem(gx + 1, GROUPS)}),
            (faces.at[t, 0], {"gx": lax.rem(gx + GROUPS - 1, GROUPS)}),
            (faces.at[t, :, 1], {"gy": lax.rem(gy + 1, OWNERS)}),
            (faces.at[t, :, 0], {"gy": lax.rem(gy + OWNERS - 1, OWNERS)}),
        ]
        return [
            pltpu.make_async_remote_copy(
                src_ref=source,
                dst_ref=halo.at[t, i],
                send_sem=halo_send.at[t, i],
                recv_sem=halo_recv.at[t, i],
                device_id=device,
                device_id_type=MESH,
            )
            for i, (source, device) in enumerate(ahead)
        ]

    def exchange(out, into, t, send_sem, recv_sem):
        def send(k, carry):
            other = lax.rem(gy + k, OWNERS)
            pltpu.make_async_remote_copy(
                src_ref=out.at[t, other],
                dst_ref=into.at[t, gy],
                send_sem=send_sem.at[t],
                recv_sem=recv_sem.at[t],
                device_id={"gy": other},
                device_id_type=MESH,
            ).start()
            return carry

        lax.fori_loop(1, OWNERS, send, 0)
        into[t, gy] = out[t, gy]

    def exchange_all(out, into, c, i, first=1, last=DEVICES):
        def send(k, carry):
            other, where = device(lax.rem(k * STRIDE, DEVICES))
            pltpu.make_async_remote_copy(
                src_ref=out.at[c, other],
                dst_ref=into.at[c, me],
                send_sem=move_send.at[i],
                recv_sem=move_recv.at[i],
                device_id=where,
                device_id_type=MESH,
            ).start()
            return carry

        lax.fori_loop(first, last, send, 0)
        if first == 1:
            into[c, me] = out[c, me]

    def await_cells(buf, c, sem):
        await_all(buf.at[c, pl.ds(0, DEVICES - 1)], sem)

    def await_all(part, sem):
        pltpu.make_async_copy(part, part, sem).wait()

    def await_row(buf, t, sem):
        await_all(buf.at[t, pl.ds(0, OWNERS - 1)], sem.at[t])

    halos = [halo_copies(t) for t in range(2)]
    for copy in halos[0]:
        copy.start()

    def iota(shape, dim):
        return lax.broadcasted_iota(jnp.int32, shape, dim)

    owner_row = jnp.concatenate([owner[q : q + 1, :] for q in range(4)], axis=1)
    label_row = jnp.concatenate([slot[q : q + 1, :] for q in range(4)], axis=1).astype(F32) + 1.0
    mine = (iota((OWNERS, CELLS), 0) == owner_row).astype(F32)
    before = (iota((CELLS, CELLS), 0) < iota((CELLS, CELLS), 1)).astype(F32)
    ahead = mat(mine.astype(BF16), before.astype(BF16))
    rank = jnp.sum(mine * ahead, axis=0, keepdims=True)
    place = owner_row.astype(F32) * HALF + rank + jnp.where(rank >= HALF, float(PLACES // 2 - HALF), 0.0)
    place = place.astype(jnp.int32)
    to_box[...] = (iota((PLACES, CELLS), 0) == place).astype(F32).astype(BF16)
    picks = (iota((CELLS, LIST), 0) == listed[...]).astype(F32)
    others = 1.0 - mat(picks.astype(BF16), jnp.ones((LIST, 128), BF16))
    later = (iota((CELLS, CELLS), 1) < iota((CELLS, CELLS), 0)).astype(F32)
    column = mat(later.astype(BF16), others.astype(BF16))
    column = jnp.where(others > 0.5, column, -1.0)[:, 0:1]
    rest = (column == iota((CELLS, LIST), 1).astype(F32)).astype(F32)
    chosen = jnp.concatenate([picks, rest], axis=1)
    order[...] = chosen.astype(BF16)
    live_row = (iota((1, LIST), 1) < count[...]).astype(F32)
    wi[...] = jnp.zeros_like(wi)
    wi[0:NS, :] = w_in[...].astype(F32)
    wo[...] = jnp.zeros_like(wo)
    wo[0:NS, :] = w_out[...].astype(F32)
    feed[...] = jnp.zeros_like(feed)
    weights_in = (0.5 * wi[...].T[:, 0:64]).astype(BF16)
    weights_hid = (0.5 * w_hid[...].astype(F32)).astype(BF16)
    weights_out = wo[...].astype(BF16)

    def mix(ref, lb, mate_of, keep=None, late=None):
        index = [mate_of[8 * o : 8 * o + 8] & 7 for o in range(4)]
        group = [mate_of[8 * o : 8 * o + 8] >> 3 for o in range(4)]

        def body(s, carry):
            base = pl.multiple_of(s * NP, NP)
            tiles = [ref[lb, pl.ds(base + 8 * g, 8), :] for g in range(4)]
            for o in range(4):
                mate = jnp.take_along_axis(tiles[0], index[o], axis=0, mode="promise_in_bounds")
                for g in range(1, 4):
                    other = jnp.take_along_axis(tiles[g], index[o], axis=0, mode="promise_in_bounds")
                    mate = jnp.where(group[o] == g, other, mate)
                mixed = 0.6 * tiles[o] + 0.4 * mate
                if keep is not None:
                    mixed = mixed * keep + r_late[late, pl.ds(s, 1), :]
                ref[lb, pl.ds(base + 8 * o, 8), :] = mixed
            return carry

        lax.fori_loop(0, NS, body, 0, unroll=2)

    def pack_cells(c, goes_c, extra):
        for j in range(14):
            if j < 13:
                value = rows_of(state, 4, 128 * j, 128)
            else:
                value = jnp.concatenate([rows_of(state, 4, 1664, 64), extra], axis=0)
            hi, lo = split(value)
            moving[c, :, j, :] = mat_nt(goes_c, hi) + mat_nt(goes_c, lo)

    def unpack_cells(c):
        for j in range(14):
            block = moved[c, :, j, :].T
            size = min(128, ROWS - 128 * j)
            guest[c, 128 * j : 128 * j + size, :] = block[0:size]
        return block[64:72], block[96:128]

    def rows_of(ref, blocks, start, size):
        return jnp.concatenate([ref[lb, start : start + size, :] for lb in range(blocks)], axis=1)

    def permute():
        for k in range(ROWS // SPAN):
            hi, lo = split(rows_of(state, 4, SPAN * k, SPAN))
            turned = mat(hi, order[...]) + mat(lo, order[...])
            for lb in range(4):
                state[lb, SPAN * k : SPAN * k + SPAN, :] = turned[:, 128 * lb : 128 * lb + 128]

    def transport(t):
        x_low = jnp.where(gx > 0, 1.0, 0.0).astype(F32)
        x_high = jnp.where(gx < GROUPS - 1, 1.0, 0.0).astype(F32)
        y_low = jnp.where(gy > 0, 1.0, 0.0).astype(F32)
        y_high = jnp.where(gy < OWNERS - 1, 1.0, 0.0).astype(F32)
        done = []
        for x in range(2):
            for y in range(2):
                center = faces[t, x, y]
                up = faces[t, 0, y] if x else halo[t, 0, y] * x_low
                down = halo[t, 1, y] * x_high if x else faces[t, 1, y]
                left = faces[t, x, 0] if y else halo[t, 2, x] * y_low
                right = halo[t, 3, x] * y_high if y else faces[t, x, 1]
                around = up + down + left + right
                around = around + pltpu.roll(center, 1, axis=1) + pltpu.roll(center, 127, axis=1)
                q = 2 * x + y
                done.append(center + 0.1 * (around - 6.0 * center) - speed[q : q + 1, :] * (center - up))
        return jnp.concatenate(done, axis=1)

    def chemistry(ref, blocks, keep, source, live):
        width = 128 * blocks
        wide = WIDE * 2 // blocks
        chains = range(CHAINS)

        def body(g, total):
            for c in chains:
                for i in range(wide):
                    p = (CHAINS * g + c) * wide + i
                    own = jnp.concatenate([ref[lb, pl.ds(p, NS, stride=NP), :] for lb in range(blocks)], axis=1)
                    feed[c * wide + i, 0:NS, 0:width] = own * keep + source[0:NS, 0:width]
            columns = [
                jnp.concatenate(
                    [
                        jnp.where(live > 0.5, feed[c * wide + i, :, 0:width], 0.0).astype(BF16)
                        for i in range(wide)
                    ],
                    axis=1,
                )
                for c in chains
            ]
            one = [silu(mat(weights_in, x)) for x in columns]
            two = [silu(mat(weights_hid, x)) for x in one]
            change = [mat(weights_out, x).astype(BF16).astype(F32) for x in two]
            for c in chains:
                for i in range(wide):
                    p = (CHAINS * g + c) * wide + i
                    part = jnp.where(live > 0.5, change[c][:, width * i : width * i + width], 0.0)
                    done = feed[c * wide + i, :, 0:width] + part
                    for lb in range(blocks):
                        ref[lb, pl.ds(p, NS, stride=NP), :] = done[0:NS, 128 * lb : 128 * lb + 128]
                    total = total + part
            return total

        return lax.fori_loop(0, NP // (CHAINS * wide), body, jnp.zeros((64, width), F32))

    def through(values, matrix, product=mat):
        hi, lo = split(values)
        both = product(jnp.concatenate([hi, lo], axis=0), matrix)
        return both[: values.shape[0]] + both[values.shape[0] :]

    for copy in loads[0:2]:
        copy.wait()
    for lb in range(2):
        mix(state, lb, partner[:, 128 * lb : 128 * lb + 128])
    row = iota((64, CELLS), 0)
    for t in range(2):
        if t == 1:
            await_cells(moved, 0, move_recv.at[0])
            await_cells(r_moved, 0, move_recv.at[2])
            meta, mate_of = unpack_cells(0)
            r_g[:, 0:128] = r_moved[0].reshape(DEVICES, 128).T[0:64]
            guest_keep, guest_live = 1.0 - meta[0:1], meta[1:2]
            guest_mates = mate_of.astype(jnp.int32)
            lands = (iota((CELLS, LIST), 0) == arrive[...]).astype(F32)
            taken = mat_nt(jnp.ones((8, LIST), BF16), lands.astype(BF16))[0:1]
            lands = lands.T
            for lb in range(4):
                turn[lb] = lands[:, 128 * lb : 128 * lb + 128]
            final[0:CELLS, :] = jnp.where(taken > 0.5, 0.0, order[...].astype(F32).T).astype(BF16)
            for c in range(2):
                final[CELLS + DEVICES * c : CELLS + DEVICES * (c + 1), :] = jnp.concatenate(
                    [turn[lb, pl.ds(c, DEVICES, stride=2), :] for lb in range(4)], axis=1
                ).astype(BF16)
        for copy in halos[t]:
            copy.wait_recv()
        grid = jnp.concatenate([transport(t), jnp.zeros((8, CELLS), F32)], axis=0)
        message = packed(to_box[...], jnp.where(row == LABEL, label_row, grid))
        for j in range(OWNERS):
            f_send[t, j] = message[HALF * j : HALF * j + HALF]
        exchange(f_send, f_recv, t, fs_sem, fr_sem)
        if t == 0:
            for copy in loads[2:4]:
                copy.wait()
            for lb in range(2, 4):
                mix(state, lb, partner[:, 128 * lb : 128 * lb + 128])
            permute()
            mates_now = mat(partner[...].astype(F32).astype(BF16), order[...])
            rate_row = through(jnp.broadcast_to(rate[...], (8, CELLS)), order[...])[0:1]
            keep_row = 1.0 - rate_row
            goes = (iota((CELLS, LIST), 0) == leave[...]).astype(F32)
            goes = mat(goes.T.astype(BF16), order[...])
            for lb in range(4):
                turn[lb] = goes[:, 128 * lb : 128 * lb + 128]
            for c in range(2):
                goes_halves[DEVICES * c : DEVICES * c + DEVICES, :] = jnp.concatenate(
                    [turn[lb, pl.ds(c, DEVICES, stride=2), :] for lb in range(4)], axis=1
                ).astype(BF16)
            live_all = jnp.concatenate([live_row, jnp.zeros((1, LIST), F32)], axis=1)
            extra = jnp.where(row == 0, rate_row, jnp.where(row == 1, live_all, 0.0))
            extra = jnp.concatenate([extra[0:32], mates_now], axis=0)
            mates[...] = extra
            pack_cells(0, goes_halves[0:DEVICES], extra)
            exchange_all(moving, moved, 0, 0, 1, EARLY)
        else:
            exchange_all(moving, moved, 1, 1, PACE[0], PACE[1])
            chemistry(guest, 1, guest_keep, r_g, guest_live)
            mix(guest, 0, guest_mates)
        await_row(f_recv, t, fr_sem)
        arrived = f_recv[t].reshape(PLACES // 2, 128)
        if t == 0:
            lane = iota((PLACES // 2, CELLS), 1).astype(F32) + 1.0
            for h in range(2):
                labels = arrived[:, 64 * h + LABEL : 64 * h + LABEL + 1]
                to_slot[h * PLACES // 2 : (h + 1) * PLACES // 2, :] = (labels == lane).astype(F32).astype(BF16)
        r_f[...] = through(unpacked(arrived, to_slot[...]), order[...]) * rate_row
        for lb in range(2):
            r_late[lb] = r_f[:, LIST + 128 * lb : LIST + 128 * lb + 128]
        hi, lo = split(r_f[...])
        both = mat_nt(goes_halves[...], jnp.concatenate([hi, lo], axis=0))
        both = both + pltpu.roll(both, 64, axis=1)
        r_moving[t, :, 0, :] = jnp.where(iota((DEVICES, 128), 1) < 64, both[:DEVICES], both[DEVICES:])
        if t == 1:
            exchange_all(r_moving, r_moved, 1, 3)
            exchange_all(moving, moved, 1, 1, PACE[1], DEVICES)
        total = chemistry(state, 2, keep_row[:, 0:LIST], r_f, live_row)
        source = through(total * (1.0 / NP), order[:, 0:LIST], mat_nt)
        message = packed(to_slot[...], source)
        for j in range(OWNERS):
            s_send[t, j] = message[HALF * j : HALF * j + HALF]
        exchange(s_send, s_recv, t, ss_sem, sr_sem)
        if t == 0:
            exchange_all(moving, moved, 0, 0, EARLY, DEVICES)
            exchange_all(r_moving, r_moved, 0, 2)
            for lb in range(4):
                cols = slice(128 * lb, 128 * lb + 128)
                mate_of = mates[32:64, cols].astype(jnp.int32)
                if lb < 2:
                    mix(state, lb, mate_of)
                else:
                    mix(state, lb, mate_of, keep_row[:, cols], lb - 2)
            pack_cells(1, goes_halves[DEVICES:], mates[...])
        else:
            def relax(s, carry):
                base = pl.multiple_of(s * NP, NP)
                for lb in range(2, 4):
                    cols = slice(128 * lb, 128 * lb + 128)
                    span = pl.ds(base, NP)
                    state[lb, span, :] = state[lb, span, :] * keep_row[:, cols] + r_late[lb - 2, pl.ds(s, 1), :]
                return carry

            lax.fori_loop(0, NS, relax, 0)
            for k in range(ROWS // SPAN):
                hi, lo = split(rows_of(state, 4, SPAN * k, SPAN))
                own = final[0:CELLS, :]
                made[SPAN * k : SPAN * k + SPAN, :] = mat(hi, own) + mat(lo, own)
            await_cells(moved, 1, move_recv.at[1])
            await_cells(r_moved, 1, move_recv.at[3])
            late_meta, _ = unpack_cells(1)
            r_turned = r_moved[1].reshape(DEVICES, 128).T
            r_g[...] = jnp.concatenate([r_turned[0:64], r_turned[64:128]], axis=1)
            guest_keep = jnp.concatenate([guest_keep, 1.0 - late_meta[0:1]], axis=1)
            guest_live = jnp.concatenate([guest_live, late_meta[1:2]], axis=1)
            chemistry(guest, 2, guest_keep, r_g, guest_live)

            stores = [
                pltpu.make_async_copy(
                    made.at[pl.ds(SPAN * k, SPAN)], parts_out.at[pl.ds(SPAN * k, SPAN)], store_sem.at[k]
                )
                for k in range(ROWS // SPAN)
            ]
            for k in range(ROWS // SPAN):
                hi, lo = split(rows_of(guest, 2, SPAN * k, SPAN))
                landing = final[CELLS:, :]
                made[SPAN * k : SPAN * k + SPAN, :] += mat(hi, landing) + mat(lo, landing)
                stores[k].start()
        await_row(s_recv, t, sr_sem)
        grid = grid + unpacked(s_recv[t].reshape(PLACES // 2, 128), to_box[...])
        if t == 0:
            for q in range(4):
                faces[1, q // 2, q % 2] = grid[0:56, 128 * q : 128 * q + 128]
            for copy in halos[1]:
                copy.start()
            exchange_all(moving, moved, 1, 1, 1, PACE[0])
        else:
            for q in range(4):
                grid_out[pl.ds(q, NS, stride=4), :] = grid[0:NS, 128 * q : 128 * q + 128]
    for copy in stores:
        copy.wait()
    for t in range(2):
        for copy in halos[t]:
            copy.wait_send()
        await_row(f_send, t, fs_sem)
        await_row(s_send, t, ss_sem)
        await_cells(moving, t, move_send.at[t])
        await_cells(r_moving, t, move_send.at[2 + t])


def per_device(
    grid_scalars, axial_speed, particles, cell_owner, cell_slot, mix_rate, partner,
    chem_input, chem_hidden, chem_output, react_slots, react_count, leave_slots, arrive_slots,
):
    vmem = pl.BlockSpec(memory_space=pltpu.VMEM)
    hbm = pl.BlockSpec(memory_space=pl.ANY)
    dma = pltpu.SemaphoreType.DMA
    messages = pltpu.VMEM((2, OWNERS, HALF, 128), F32)
    cells = pltpu.VMEM((2, DEVICES, 14, 128), F32)
    short = pltpu.VMEM((2, DEVICES, 1, 128), F32)
    grid, out = pl.pallas_call(
        step_kernel,
        out_shape=(
            jax.ShapeDtypeStruct((4 * NS, 128), F32),
            jax.ShapeDtypeStruct((ROWS, CELLS), F32),
        ),
        in_specs=[vmem, vmem, hbm] + [vmem] * 11,
        out_specs=(vmem, hbm),
        scratch_shapes=[
            pltpu.VMEM((4, ROWS, 128), F32),
            pltpu.VMEM((2, ROWS, 128), F32),
            pltpu.VMEM((2, 2, 2, 56, 128), F32),
            pltpu.VMEM((2, 4, 2, 56, 128), F32),
            messages,
            messages,
            messages,
            messages,
            cells,
            cells,
            short,
            short,
            pltpu.VMEM((PLACES, CELLS), BF16),
            pltpu.VMEM((PLACES, CELLS), BF16),
            pltpu.VMEM((CELLS, CELLS), BF16),
            pltpu.VMEM((CELLS + LIST, CELLS), BF16),
            pltpu.VMEM((4, LIST, 128), F32),
            pltpu.VMEM((LIST, CELLS), BF16),
            pltpu.VMEM((64, CELLS), F32),
            pltpu.VMEM((CHAINS * WIDE * 2, 64, LIST), F32),
            pltpu.VMEM((64, CELLS), F32),
            pltpu.VMEM((2, 64, 128), F32),
            pltpu.VMEM((64, LIST), F32),
            pltpu.VMEM((ROWS, CELLS), F32),
            pltpu.VMEM((128, 256), F32),
            pltpu.VMEM((64, 256), F32),
            dma((4,)),
            dma((ROWS // SPAN,)),
            dma((2, 4)),
            dma((2, 4)),
            dma((2,)),
            dma((2,)),
            dma((2,)),
            dma((2,)),
            dma((4,)),
            dma((4,)),
        ],
        compiler_params=pltpu.CompilerParams(
            collective_id=0, has_side_effects=True, vmem_limit_bytes=VMEM_LIMIT
        ),
        name="step",
    )(
        grid_scalars.reshape(4 * NS, 128),
        axial_speed.reshape(4, 128),
        particles.reshape(ROWS, CELLS),
        cell_owner.reshape(4, 128),
        cell_slot.reshape(4, 128),
        mix_rate.reshape(1, CELLS),
        partner,
        chem_input.T,
        chem_hidden,
        chem_output,
        react_slots,
        react_count.reshape(1, 1),
        leave_slots,
        arrive_slots,
    )
    return grid.reshape(grid_scalars.shape), out.reshape(particles.shape)


def solution(mesh):
    placed = (
        P(None, "gx", "gy", None),
        P("gx", "gy", None),
        P(None, None, ("gx", "gy")),
        P("gx", "gy", None),
        P("gx", "gy", None),
        P(("gx", "gy")),
        P(None, ("gx", "gy")),
        P(),
        P(),
        P(),
        P(("gx", "gy"), None),
        P(("gx", "gy")),
        P(("gx", "gy"), None),
        P(("gx", "gy"), None),
    )
    return jax.shard_map(
        per_device,
        mesh=mesh,
        in_specs=placed,
        out_specs=(P(None, "gx", "gy", None), P(None, None, ("gx", "gy"))),
        check_vma=False,
    )
```

```python
import functools

import jax
import jax.numpy as jnp
from jax import lax
from jax.experimental import pallas as pl
from jax.experimental.pallas import tpu as pltpu
from jax.sharding import PartitionSpec as P

F32, BF16 = jnp.float32, jnp.bfloat16
MESH = pl.DeviceIdType.MESH

NS, NP, CELLS = 54, 32, 512
ROWS = NS * NP
OWNERS, GROUPS, DEVICES = 32, 4, 128
HALF = 16
PLACES = 2 * OWNERS * HALF
LIST = 256
SPAN = 432
STRIDE = 43
EARLY = 110
PACE = (20, 70)
CHAINS, WIDE = 2, 4
LABEL = 54
VMEM_LIMIT = 56 * 1024 * 1024
NT = (((1,), (1,)), ((), ()))


def split(x):
    hi = x.astype(BF16)
    return hi, (x - hi.astype(F32)).astype(BF16)


def mat(a, b):
    return jnp.dot(a, b, preferred_element_type=F32)


def mat_nt(a, b):
    return lax.dot_general(a, b, NT, preferred_element_type=F32)


def silu(a):
    return (a + a * jnp.tanh(a)).astype(BF16)


def packed(picker, values):
    hi, lo = split(values)
    both = mat_nt(picker, jnp.concatenate([hi, lo], axis=0))
    both = both + pltpu.roll(both, 64, axis=1)
    lane = lax.broadcasted_iota(jnp.int32, (PLACES // 2, 128), 1)
    return jnp.where(lane < 64, both[: PLACES // 2], both[PLACES // 2 :])


def unpacked(message, placer):
    turned = message.T
    values = jnp.concatenate([turned[:64], turned[64:]], axis=1)
    hi, lo = split(values)
    both = mat(jnp.concatenate([hi, lo], axis=0), placer)
    return both[:64] + both[64:]


def step_kernel(
    grid_in, speed, parts_in, owner, slot, rate, partner, w_in, w_hid, w_out, listed, count, leave, arrive,
    grid_out, parts_out,
    state, guest, faces, halo, f_send, f_recv, s_send, s_recv, moving, moved, r_moving, r_moved,
    to_box, to_slot, order, final, turn, goes_halves, mates, feed, r_f, r_late, r_g, made, wi, wo,
    load_sem, store_sem, halo_send, halo_recv, fs_sem, fr_sem, ss_sem, sr_sem, move_send, move_recv,
):
    gx, gy = lax.axis_index("gx"), lax.axis_index("gy")
    me = gx * OWNERS + gy
    barrier = pltpu.get_barrier_semaphore()

    loads = [
        pltpu.make_async_copy(parts_in.at[:, pl.ds(128 * lb, 128)], state.at[lb], load_sem.at[lb]) for lb in range(4)
    ]
    for copy in loads:
        copy.start()

    def device(k):
        other = lax.rem(me + k, DEVICES)
        return other, {"gx": other // OWNERS, "gy": lax.rem(other, OWNERS)}

    def greet(k, carry):
        pl.semaphore_signal(barrier, inc=1, device_id=device(k)[1], device_id_type=MESH)
        return carry

    lax.fori_loop(1, DEVICES, greet, 0)

    for q in range(4):
        faces[0, q // 2, q % 2, 0:NS, :] = grid_in[pl.ds(q, NS, stride=4), :]
        faces[0, q // 2, q % 2, NS:56, :] = jnp.zeros((56 - NS, 128), F32)

    pl.semaphore_wait(barrier, DEVICES - 1)

    def halo_copies(t):
        ahead = [
            (faces.at[t, 1], {"gx": lax.rem(gx + 1, GROUPS)}),
            (faces.at[t, 0], {"gx": lax.rem(gx + GROUPS - 1, GROUPS)}),
            (faces.at[t, :, 1], {"gy": lax.rem(gy + 1, OWNERS)}),
            (faces.at[t, :, 0], {"gy": lax.rem(gy + OWNERS - 1, OWNERS)}),
        ]
        return [
            pltpu.make_async_remote_copy(
                src_ref=source,
                dst_ref=halo.at[t, i],
                send_sem=halo_send.at[t, i],
                recv_sem=halo_recv.at[t, i],
                device_id=device,
                device_id_type=MESH,
            )
            for i, (source, device) in enumerate(ahead)
        ]

    def exchange(out, into, t, send_sem, recv_sem):
        def send(k, carry):
            other = lax.rem(gy + k, OWNERS)
            pltpu.make_async_remote_copy(
                src_ref=out.at[t, other],
                dst_ref=into.at[t, gy],
                send_sem=send_sem.at[t],
                recv_sem=recv_sem.at[t],
                device_id={"gy": other},
                device_id_type=MESH,
            ).start()
            return carry

        lax.fori_loop(1, OWNERS, send, 0)
        into[t, gy] = out[t, gy]

    def exchange_all(out, into, c, i, first=1, last=DEVICES):
        def send(k, carry):
            other, where = device(lax.rem(k * STRIDE, DEVICES))
            pltpu.make_async_remote_copy(
                src_ref=out.at[c, other],
                dst_ref=into.at[c, me],
                send_sem=move_send.at[i],
                recv_sem=move_recv.at[i],
                device_id=where,
                device_id_type=MESH,
            ).start()
            return carry

        lax.fori_loop(first, last, send, 0)
        if first == 1:
            into[c, me] = out[c, me]

    def await_cells(buf, c, sem):
        await_all(buf.at[c, pl.ds(0, DEVICES - 1)], sem)

    def await_all(part, sem):
        pltpu.make_async_copy(part, part, sem).wait()

    def await_row(buf, t, sem):
        await_all(buf.at[t, pl.ds(0, OWNERS - 1)], sem.at[t])

    halos = [halo_copies(t) for t in range(2)]
    for copy in halos[0]:
        copy.start()

    def iota(shape, dim):
        return lax.broadcasted_iota(jnp.int32, shape, dim)

    owner_row = jnp.concatenate([owner[q : q + 1, :] for q in range(4)], axis=1)
    label_row = jnp.concatenate([slot[q : q + 1, :] for q in range(4)], axis=1).astype(F32) + 1.0
    mine = (iota((OWNERS, CELLS), 0) == owner_row).astype(F32)
    before = (iota((CELLS, CELLS), 0) < iota((CELLS, CELLS), 1)).astype(F32)
    ahead = mat(mine.astype(BF16), before.astype(BF16))
    rank = jnp.sum(mine * ahead, axis=0, keepdims=True)
    place = owner_row.astype(F32) * HALF + rank + jnp.where(rank >= HALF, float(PLACES // 2 - HALF), 0.0)
    place = place.astype(jnp.int32)
    to_box[...] = (iota((PLACES, CELLS), 0) == place).astype(F32).astype(BF16)
    picks = (iota((CELLS, LIST), 0) == listed[...]).astype(F32)
    others = 1.0 - mat(picks.astype(BF16), jnp.ones((LIST, 128), BF16))
    later = (iota((CELLS, CELLS), 1) < iota((CELLS, CELLS), 0)).astype(F32)
    column = mat(later.astype(BF16), others.astype(BF16))
    column = jnp.where(others > 0.5, column, -1.0)[:, 0:1]
    rest = (column == iota((CELLS, LIST), 1).astype(F32)).astype(F32)
    chosen = jnp.concatenate([picks, rest], axis=1)
    order[...] = chosen.astype(BF16)
    live_row = (iota((1, LIST), 1) < count[...]).astype(F32)
    wi[...] = jnp.zeros_like(wi)
    wi[0:NS, :] = w_in[...].astype(F32)
    wo[...] = jnp.zeros_like(wo)
    wo[0:NS, :] = w_out[...].astype(F32)
    feed[...] = jnp.zeros_like(feed)
    weights_in = (0.5 * wi[...].T[:, 0:64]).astype(BF16)
    weights_hid = (0.5 * w_hid[...].astype(F32)).astype(BF16)
    weights_out = wo[...].astype(BF16)

    def mix(ref, lb, mate_of, keep=None, late=None):
        index = [mate_of[8 * o : 8 * o + 8] & 7 for o in range(4)]
        group = [mate_of[8 * o : 8 * o + 8] >> 3 for o in range(4)]

        def body(s, carry):
            base = pl.multiple_of(s * NP, NP)
            tiles = [ref[lb, pl.ds(base + 8 * g, 8), :] for g in range(4)]
            for o in range(4):
                mate = jnp.take_along_axis(tiles[0], index[o], axis=0, mode="promise_in_bounds")
                for g in range(1, 4):
                    other = jnp.take_along_axis(tiles[g], index[o], axis=0, mode="promise_in_bounds")
                    mate = jnp.where(group[o] == g, other, mate)
                mixed = 0.6 * tiles[o] + 0.4 * mate
                if keep is not None:
                    mixed = mixed * keep + r_late[late, pl.ds(s, 1), :]
                ref[lb, pl.ds(base + 8 * o, 8), :] = mixed
            return carry

        lax.fori_loop(0, NS, body, 0, unroll=2)

    def pack_cells(c, goes_c, extra):
        for j in range(14):
            if j < 13:
                value = rows_of(state, 4, 128 * j, 128)
            else:
                value = jnp.concatenate([rows_of(state, 4, 1664, 64), extra], axis=0)
            hi, lo = split(value)
            moving[c, :, j, :] = mat_nt(goes_c, hi) + mat_nt(goes_c, lo)

    def unpack_cells(c):
        for j in range(14):
            block = moved[c, :, j, :].T
            size = min(128, ROWS - 128 * j)
            guest[c, 128 * j : 128 * j + size, :] = block[0:size]
        return block[64:72], block[96:128]

    def rows_of(ref, blocks, start, size):
        return jnp.concatenate([ref[lb, start : start + size, :] for lb in range(blocks)], axis=1)

    def permute():
        for k in range(ROWS // SPAN):
            hi, lo = split(rows_of(state, 4, SPAN * k, SPAN))
            turned = mat(hi, order[...]) + mat(lo, order[...])
            for lb in range(4):
                state[lb, SPAN * k : SPAN * k + SPAN, :] = turned[:, 128 * lb : 128 * lb + 128]

    def transport(t):
        x_low = jnp.where(gx > 0, 1.0, 0.0).astype(F32)
        x_high = jnp.where(gx < GROUPS - 1, 1.0, 0.0).astype(F32)
        y_low = jnp.where(gy > 0, 1.0, 0.0).astype(F32)
        y_high = jnp.where(gy < OWNERS - 1, 1.0, 0.0).astype(F32)
        done = []
        for x in range(2):
            for y in range(2):
                center = faces[t, x, y]
                up = faces[t, 0, y] if x else halo[t, 0, y] * x_low
                down = halo[t, 1, y] * x_high if x else faces[t, 1, y]
                left = faces[t, x, 0] if y else halo[t, 2, x] * y_low
                right = halo[t, 3, x] * y_high if y else faces[t, x, 1]
                around = up + down + left + right
                around = around + pltpu.roll(center, 1, axis=1) + pltpu.roll(center, 127, axis=1)
                q = 2 * x + y
                done.append(center + 0.1 * (around - 6.0 * center) - speed[q : q + 1, :] * (center - up))
        return jnp.concatenate(done, axis=1)

    def chemistry(ref, blocks, keep, source, live):
        width = 128 * blocks
        wide = WIDE * 2 // blocks
        chains = range(CHAINS)

        def body(g, total):
            for c in chains:
                for i in range(wide):
                    p = (CHAINS * g + c) * wide + i
                    own = jnp.concatenate([ref[lb, pl.ds(p, NS, stride=NP), :] for lb in range(blocks)], axis=1)
                    feed[c * wide + i, 0:NS, 0:width] = own * keep + source[0:NS, 0:width]
            columns = [
                jnp.concatenate(
                    [
                        jnp.where(live > 0.5, feed[c * wide + i, :, 0:width], 0.0).astype(BF16)
                        for i in range(wide)
                    ],
                    axis=1,
                )
                for c in chains
            ]
            one = [silu(mat(weights_in, x)) for x in columns]
            two = [silu(mat(weights_hid, x)) for x in one]
            change = [mat(weights_out, x).astype(BF16).astype(F32) for x in two]
            for c in chains:
                for i in range(wide):
                    p = (CHAINS * g + c) * wide + i
                    part = jnp.where(live > 0.5, change[c][:, width * i : width * i + width], 0.0)
                    done = feed[c * wide + i, :, 0:width] + part
                    for lb in range(blocks):
                        ref[lb, pl.ds(p, NS, stride=NP), :] = done[0:NS, 128 * lb : 128 * lb + 128]
                    total = total + part
            return total

        return lax.fori_loop(0, NP // (CHAINS * wide), body, jnp.zeros((64, width), F32))

    def through(values, matrix, product=mat):
        hi, lo = split(values)
        both = product(jnp.concatenate([hi, lo], axis=0), matrix)
        return both[: values.shape[0]] + both[values.shape[0] :]

    for copy in loads[0:2]:
        copy.wait()
    for lb in range(2):
        mix(state, lb, partner[:, 128 * lb : 128 * lb + 128])
    def with_source(grid, t):
        await_row(s_recv, t, sr_sem)
        return grid + unpacked(s_recv[t].reshape(PLACES // 2, 128), to_box[...])

    row = iota((64, CELLS), 0)
    for t in range(2):
        if t == 1:
            await_cells(moved, 0, move_recv.at[0])
            await_cells(r_moved, 0, move_recv.at[2])
            meta, mate_of = unpack_cells(0)
            r_g[:, 0:128] = r_moved[0].reshape(DEVICES, 128).T[0:64]
            guest_keep, guest_live = 1.0 - meta[0:1], meta[1:2]
            guest_mates = mate_of.astype(jnp.int32)
            lands = (iota((CELLS, LIST), 0) == arrive[...]).astype(F32)
            taken = mat_nt(jnp.ones((8, LIST), BF16), lands.astype(BF16))[0:1]
            lands = lands.T
            for lb in range(4):
                turn[lb] = lands[:, 128 * lb : 128 * lb + 128]
            final[0:CELLS, :] = jnp.where(taken > 0.5, 0.0, order[...].astype(F32).T).astype(BF16)
            for c in range(2):
                final[CELLS + DEVICES * c : CELLS + DEVICES * (c + 1), :] = jnp.concatenate(
                    [turn[lb, pl.ds(c, DEVICES, stride=2), :] for lb in range(4)], axis=1
                ).astype(BF16)
        for copy in halos[t]:
            copy.wait_recv()
        grid = jnp.concatenate([transport(t), jnp.zeros((8, CELLS), F32)], axis=0)
        message = packed(to_box[...], jnp.where(row == LABEL, label_row, grid))
        for j in range(OWNERS):
            f_send[t, j] = message[HALF * j : HALF * j + HALF]
        exchange(f_send, f_recv, t, fs_sem, fr_sem)
        if t == 0:
            for copy in loads[2:4]:
                copy.wait()
            for lb in range(2, 4):
                mix(state, lb, partner[:, 128 * lb : 128 * lb + 128])
            permute()
            mates_now = mat(partner[...].astype(F32).astype(BF16), order[...])
            rate_row = through(jnp.broadcast_to(rate[...], (8, CELLS)), order[...])[0:1]
            keep_row = 1.0 - rate_row
            goes = (iota((CELLS, LIST), 0) == leave[...]).astype(F32)
            goes = mat(goes.T.astype(BF16), order[...])
            for lb in range(4):
                turn[lb] = goes[:, 128 * lb : 128 * lb + 128]
            for c in range(2):
                goes_halves[DEVICES * c : DEVICES * c + DEVICES, :] = jnp.concatenate(
                    [turn[lb, pl.ds(c, DEVICES, stride=2), :] for lb in range(4)], axis=1
                ).astype(BF16)
            live_all = jnp.concatenate([live_row, jnp.zeros((1, LIST), F32)], axis=1)
            extra = jnp.where(row == 0, rate_row, jnp.where(row == 1, live_all, 0.0))
            extra = jnp.concatenate([extra[0:32], mates_now], axis=0)
            mates[...] = extra
            pack_cells(0, goes_halves[0:DEVICES], extra)
            exchange_all(moving, moved, 0, 0, 1, EARLY)
        else:
            exchange_all(moving, moved, 1, 1, PACE[0], PACE[1])
            chemistry(guest, 1, guest_keep, r_g, guest_live)
            mix(guest, 0, guest_mates)
        await_row(f_recv, t, fr_sem)
        arrived = f_recv[t].reshape(PLACES // 2, 128)
        if t == 0:
            lane = iota((PLACES // 2, CELLS), 1).astype(F32) + 1.0
            for h in range(2):
                labels = arrived[:, 64 * h + LABEL : 64 * h + LABEL + 1]
                to_slot[h * PLACES // 2 : (h + 1) * PLACES // 2, :] = (labels == lane).astype(F32).astype(BF16)
        r_f[...] = through(unpacked(arrived, to_slot[...]), order[...]) * rate_row
        for lb in range(2):
            r_late[lb] = r_f[:, LIST + 128 * lb : LIST + 128 * lb + 128]
        hi, lo = split(r_f[...])
        both = mat_nt(goes_halves[...], jnp.concatenate([hi, lo], axis=0))
        both = both + pltpu.roll(both, 64, axis=1)
        r_moving[t, :, 0, :] = jnp.where(iota((DEVICES, 128), 1) < 64, both[:DEVICES], both[DEVICES:])
        if t == 1:
            exchange_all(r_moving, r_moved, 1, 3)
            exchange_all(moving, moved, 1, 1, PACE[1], DEVICES)
        total = chemistry(state, 2, keep_row[:, 0:LIST], r_f, live_row)
        source = through(total * (1.0 / NP), order[:, 0:LIST], mat_nt)
        message = packed(to_slot[...], source)
        for j in range(OWNERS):
            s_send[t, j] = message[HALF * j : HALF * j + HALF]
        exchange(s_send, s_recv, t, ss_sem, sr_sem)
        if t == 0:
            exchange_all(moving, moved, 0, 0, EARLY, DEVICES)
            exchange_all(r_moving, r_moved, 0, 2)
            for lb in range(4):
                cols = slice(128 * lb, 128 * lb + 128)
                mate_of = mates[32:64, cols].astype(jnp.int32)
                if lb < 2:
                    mix(state, lb, mate_of)
                else:
                    mix(state, lb, mate_of, keep_row[:, cols], lb - 2)
            pack_cells(1, goes_halves[DEVICES:], mates[...])
        else:
            def relax(s, carry):
                base = pl.multiple_of(s * NP, NP)
                for lb in range(2, 4):
                    cols = slice(128 * lb, 128 * lb + 128)
                    span = pl.ds(base, NP)
                    state[lb, span, :] = state[lb, span, :] * keep_row[:, cols] + r_late[lb - 2, pl.ds(s, 1), :]
                return carry

            lax.fori_loop(0, NS, relax, 0)
            for k in range(ROWS // SPAN):
                hi, lo = split(rows_of(state, 4, SPAN * k, SPAN))
                own = final[0:CELLS, :]
                made[SPAN * k : SPAN * k + SPAN, :] = mat(hi, own) + mat(lo, own)
            grid = with_source(grid, t)
            for q in range(4):
                grid_out[pl.ds(q, NS, stride=4), :] = grid[0:NS, 128 * q : 128 * q + 128]
            await_cells(moved, 1, move_recv.at[1])
            await_cells(r_moved, 1, move_recv.at[3])
            late_meta, _ = unpack_cells(1)
            r_turned = r_moved[1].reshape(DEVICES, 128).T
            r_g[...] = jnp.concatenate([r_turned[0:64], r_turned[64:128]], axis=1)
            guest_keep = jnp.concatenate([guest_keep, 1.0 - late_meta[0:1]], axis=1)
            guest_live = jnp.concatenate([guest_live, late_meta[1:2]], axis=1)
            chemistry(guest, 2, guest_keep, r_g, guest_live)

            stores = [
                pltpu.make_async_copy(
                    made.at[pl.ds(SPAN * k, SPAN)], parts_out.at[pl.ds(SPAN * k, SPAN)], store_sem.at[k]
                )
                for k in range(ROWS // SPAN)
            ]
            for k in range(ROWS // SPAN):
                hi, lo = split(rows_of(guest, 2, SPAN * k, SPAN))
                landing = final[CELLS:, :]
                made[SPAN * k : SPAN * k + SPAN, :] += mat(hi, landing) + mat(lo, landing)
                stores[k].start()
        if t == 0:
            grid = with_source(grid, t)
            for q in range(4):
                faces[1, q // 2, q % 2] = grid[0:56, 128 * q : 128 * q + 128]
            for copy in halos[1]:
                copy.start()
            exchange_all(moving, moved, 1, 1, 1, PACE[0])
    for copy in stores:
        copy.wait()
    for t in range(2):
        for copy in halos[t]:
            copy.wait_send()
        await_row(f_send, t, fs_sem)
        await_row(s_send, t, ss_sem)
        await_cells(moving, t, move_send.at[t])
        await_cells(r_moving, t, move_send.at[2 + t])


def per_device(
    grid_scalars, axial_speed, particles, cell_owner, cell_slot, mix_rate, partner,
    chem_input, chem_hidden, chem_output, react_slots, react_count, leave_slots, arrive_slots,
):
    vmem = pl.BlockSpec(memory_space=pltpu.VMEM)
    hbm = pl.BlockSpec(memory_space=pl.ANY)
    dma = pltpu.SemaphoreType.DMA
    messages = pltpu.VMEM((2, OWNERS, HALF, 128), F32)
    cells = pltpu.VMEM((2, DEVICES, 14, 128), F32)
    short = pltpu.VMEM((2, DEVICES, 1, 128), F32)
    grid, out = pl.pallas_call(
        step_kernel,
        out_shape=(
            jax.ShapeDtypeStruct((4 * NS, 128), F32),
            jax.ShapeDtypeStruct((ROWS, CELLS), F32),
        ),
        in_specs=[vmem, vmem, hbm] + [vmem] * 11,
        out_specs=(vmem, hbm),
        scratch_shapes=[
            pltpu.VMEM((4, ROWS, 128), F32),
            pltpu.VMEM((2, ROWS, 128), F32),
            pltpu.VMEM((2, 2, 2, 56, 128), F32),
            pltpu.VMEM((2, 4, 2, 56, 128), F32),
            messages,
            messages,
            messages,
            messages,
            cells,
            cells,
            short,
            short,
            pltpu.VMEM((PLACES, CELLS), BF16),
            pltpu.VMEM((PLACES, CELLS), BF16),
            pltpu.VMEM((CELLS, CELLS), BF16),
            pltpu.VMEM((CELLS + LIST, CELLS), BF16),
            pltpu.VMEM((4, LIST, 128), F32),
            pltpu.VMEM((LIST, CELLS), BF16),
            pltpu.VMEM((64, CELLS), F32),
            pltpu.VMEM((CHAINS * WIDE * 2, 64, LIST), F32),
            pltpu.VMEM((64, CELLS), F32),
            pltpu.VMEM((2, 64, 128), F32),
            pltpu.VMEM((64, LIST), F32),
            pltpu.VMEM((ROWS, CELLS), F32),
            pltpu.VMEM((128, 256), F32),
            pltpu.VMEM((64, 256), F32),
            dma((4,)),
            dma((ROWS // SPAN,)),
            dma((2, 4)),
            dma((2, 4)),
            dma((2,)),
            dma((2,)),
            dma((2,)),
            dma((2,)),
            dma((4,)),
            dma((4,)),
        ],
        compiler_params=pltpu.CompilerParams(
            collective_id=0, has_side_effects=True, vmem_limit_bytes=VMEM_LIMIT
        ),
        name="step",
    )(
        grid_scalars.reshape(4 * NS, 128),
        axial_speed.reshape(4, 128),
        particles.reshape(ROWS, CELLS),
        cell_owner.reshape(4, 128),
        cell_slot.reshape(4, 128),
        mix_rate.reshape(1, CELLS),
        partner,
        chem_input.T,
        chem_hidden,
        chem_output,
        react_slots,
        react_count.reshape(1, 1),
        leave_slots,
        arrive_slots,
    )
    return grid.reshape(grid_scalars.shape), out.reshape(particles.shape)


def solution(mesh):
    placed = (
        P(None, "gx", "gy", None),
        P("gx", "gy", None),
        P(None, None, ("gx", "gy")),
        P("gx", "gy", None),
        P("gx", "gy", None),
        P(("gx", "gy")),
        P(None, ("gx", "gy")),
        P(),
        P(),
        P(),
        P(("gx", "gy"), None),
        P(("gx", "gy")),
        P(("gx", "gy"), None),
        P(("gx", "gy"), None),
    )
    return jax.shard_map(
        per_device,
        mesh=mesh,
        in_specs=placed,
        out_specs=(P(None, "gx", "gy", None), P(None, None, ("gx", "gy"))),
        check_vma=False,
    )
```

```python
import functools

import jax
import jax.numpy as jnp
from jax import lax
from jax.experimental import pallas as pl
from jax.experimental.pallas import tpu as pltpu
from jax.sharding import PartitionSpec as P

F32, BF16 = jnp.float32, jnp.bfloat16
MESH = pl.DeviceIdType.MESH

NS, NP, CELLS = 54, 32, 512
ROWS = NS * NP
OWNERS, GROUPS, DEVICES = 32, 4, 128
HALF = 16
PLACES = 2 * OWNERS * HALF
LIST = 256
SPAN = 432
STRIDE = 43
EARLY = 110
PACE = (20, 70)
CHAINS, WIDE = 2, 4
LABEL = 54
VMEM_LIMIT = 56 * 1024 * 1024
NT = (((1,), (1,)), ((), ()))


def split(x):
    hi = x.astype(BF16)
    return hi, (x - hi.astype(F32)).astype(BF16)


def mat(a, b):
    return jnp.dot(a, b, preferred_element_type=F32)


def mat_nt(a, b):
    return lax.dot_general(a, b, NT, preferred_element_type=F32)


def silu(a):
    return (a + a * jnp.tanh(a)).astype(BF16)


def packed(picker, values):
    hi, lo = split(values)
    both = mat_nt(picker, jnp.concatenate([hi, lo], axis=0))
    both = both + pltpu.roll(both, 64, axis=1)
    lane = lax.broadcasted_iota(jnp.int32, (PLACES // 2, 128), 1)
    return jnp.where(lane < 64, both[: PLACES // 2], both[PLACES // 2 :])


def unpacked(message, placer):
    turned = message.T
    values = jnp.concatenate([turned[:64], turned[64:]], axis=1)
    hi, lo = split(values)
    both = mat(jnp.concatenate([hi, lo], axis=0), placer)
    return both[:64] + both[64:]


def step_kernel(
    grid_in, speed, parts_in, owner, slot, rate, partner, w_in, w_hid, w_out, listed, count, leave, arrive,
    grid_out, parts_out,
    state, guest, faces, halo, f_send, f_recv, s_send, s_recv, moving, moved, r_moving, r_moved,
    to_box, to_slot, order, final, turn, goes_halves, mates, feed, r_f, r_late, r_g, made, wi, wo,
    load_sem, store_sem, halo_send, halo_recv, fs_sem, fr_sem, ss_sem, sr_sem, move_send, move_recv,
):
    gx, gy = lax.axis_index("gx"), lax.axis_index("gy")
    me = gx * OWNERS + gy
    barrier = pltpu.get_barrier_semaphore()

    loads = [
        pltpu.make_async_copy(parts_in.at[:, pl.ds(128 * lb, 128)], state.at[lb], load_sem.at[lb]) for lb in range(4)
    ]
    for copy in loads:
        copy.start()

    def device(k):
        other = lax.rem(me + k, DEVICES)
        return other, {"gx": other // OWNERS, "gy": lax.rem(other, OWNERS)}

    def greet(k, carry):
        pl.semaphore_signal(barrier, inc=1, device_id=device(k)[1], device_id_type=MESH)
        return carry

    lax.fori_loop(1, DEVICES, greet, 0)

    for q in range(4):
        faces[0, q // 2, q % 2, 0:NS, :] = grid_in[pl.ds(q, NS, stride=4), :]
        faces[0, q // 2, q % 2, NS:56, :] = jnp.zeros((56 - NS, 128), F32)

    pl.semaphore_wait(barrier, DEVICES - 1)

    def halo_copies(t):
        ahead = [
            (faces.at[t, 1], {"gx": lax.rem(gx + 1, GROUPS)}),
            (faces.at[t, 0], {"gx": lax.rem(gx + GROUPS - 1, GROUPS)}),
            (faces.at[t, :, 1], {"gy": lax.rem(gy + 1, OWNERS)}),
            (faces.at[t, :, 0], {"gy": lax.rem(gy + OWNERS - 1, OWNERS)}),
        ]
        return [
            pltpu.make_async_remote_copy(
                src_ref=source,
                dst_ref=halo.at[t, i],
                send_sem=halo_send.at[t, i],
                recv_sem=halo_recv.at[t, i],
                device_id=device,
                device_id_type=MESH,
            )
            for i, (source, device) in enumerate(ahead)
        ]

    def exchange(out, into, t, send_sem, recv_sem):
        def send(k, carry):
            other = lax.rem(gy + k, OWNERS)
            pltpu.make_async_remote_copy(
                src_ref=out.at[t, other],
                dst_ref=into.at[t, gy],
                send_sem=send_sem.at[t],
                recv_sem=recv_sem.at[t],
                device_id={"gy": other},
                device_id_type=MESH,
            ).start()
            return carry

        lax.fori_loop(1, OWNERS, send, 0)
        into[t, gy] = out[t, gy]

    def exchange_all(out, into, c, i, first=1, last=DEVICES):
        def send(k, carry):
            other, where = device(lax.rem(k * STRIDE, DEVICES))
            pltpu.make_async_remote_copy(
                src_ref=out.at[c, other],
                dst_ref=into.at[c, me],
                send_sem=move_send.at[i],
                recv_sem=move_recv.at[i],
                device_id=where,
                device_id_type=MESH,
            ).start()
            return carry

        lax.fori_loop(first, last, send, 0)
        if first == 1:
            into[c, me] = out[c, me]

    def await_cells(buf, c, sem):
        await_all(buf.at[c, pl.ds(0, DEVICES - 1)], sem)

    def await_all(part, sem):
        pltpu.make_async_copy(part, part, sem).wait()

    def await_row(buf, t, sem):
        await_all(buf.at[t, pl.ds(0, OWNERS - 1)], sem.at[t])

    halos = [halo_copies(t) for t in range(2)]
    for copy in halos[0]:
        copy.start()

    def iota(shape, dim):
        return lax.broadcasted_iota(jnp.int32, shape, dim)

    owner_row = jnp.concatenate([owner[q : q + 1, :] for q in range(4)], axis=1)
    label_row = jnp.concatenate([slot[q : q + 1, :] for q in range(4)], axis=1).astype(F32) + 1.0
    mine = (iota((OWNERS, CELLS), 0) == owner_row).astype(F32)
    before = (iota((CELLS, CELLS), 0) < iota((CELLS, CELLS), 1)).astype(F32)
    ahead = mat(mine.astype(BF16), before.astype(BF16))
    rank = jnp.sum(mine * ahead, axis=0, keepdims=True)
    place = owner_row.astype(F32) * HALF + rank + jnp.where(rank >= HALF, float(PLACES // 2 - HALF), 0.0)
    place = place.astype(jnp.int32)
    to_box[...] = (iota((PLACES, CELLS), 0) == place).astype(F32).astype(BF16)
    picks = (iota((CELLS, LIST), 0) == listed[...]).astype(F32)
    others = 1.0 - mat(picks.astype(BF16), jnp.ones((LIST, 128), BF16))
    later = (iota((CELLS, CELLS), 1) < iota((CELLS, CELLS), 0)).astype(F32)
    column = mat(later.astype(BF16), others.astype(BF16))
    column = jnp.where(others > 0.5, column, -1.0)[:, 0:1]
    rest = (column == iota((CELLS, LIST), 1).astype(F32)).astype(F32)
    chosen = jnp.concatenate([picks, rest], axis=1)
    order[...] = chosen.astype(BF16)
    live_row = (iota((1, LIST), 1) < count[...]).astype(F32)
    wi[...] = jnp.zeros_like(wi)
    wi[0:NS, :] = w_in[...].astype(F32)
    wo[...] = jnp.zeros_like(wo)
    wo[0:NS, :] = w_out[...].astype(F32)
    feed[...] = jnp.zeros_like(feed)
    weights_in = (0.5 * wi[...].T[:, 0:64]).astype(BF16)
    weights_hid = (0.5 * w_hid[...].astype(F32)).astype(BF16)
    weights_out = wo[...].astype(BF16)

    def mix(ref, lb, mate_of, keep=None, late=None):
        index = [mate_of[8 * o : 8 * o + 8] & 7 for o in range(4)]
        group = [mate_of[8 * o : 8 * o + 8] >> 3 for o in range(4)]

        def body(s, carry):
            base = pl.multiple_of(s * NP, NP)
            tiles = [ref[lb, pl.ds(base + 8 * g, 8), :] for g in range(4)]
            for o in range(4):
                mate = jnp.take_along_axis(tiles[0], index[o], axis=0, mode="promise_in_bounds")
                for g in range(1, 4):
                    other = jnp.take_along_axis(tiles[g], index[o], axis=0, mode="promise_in_bounds")
                    mate = jnp.where(group[o] == g, other, mate)
                mixed = 0.6 * tiles[o] + 0.4 * mate
                if keep is not None:
                    mixed = mixed * keep + r_late[late, pl.ds(s, 1), :]
                ref[lb, pl.ds(base + 8 * o, 8), :] = mixed
            return carry

        lax.fori_loop(0, NS, body, 0, unroll=2)

    def pack_cells(c, goes_c, extra):
        for j in range(14):
            if j < 13:
                value = rows_of(state, 4, 128 * j, 128)
            else:
                value = jnp.concatenate([rows_of(state, 4, 1664, 64), extra], axis=0)
            hi, lo = split(value)
            moving[c, :, j, :] = mat_nt(goes_c, hi) + mat_nt(goes_c, lo)

    def unpack_cells(c):
        for j in range(14):
            block = moved[c, :, j, :].T
            size = min(128, ROWS - 128 * j)
            guest[c, 128 * j : 128 * j + size, :] = block[0:size]
        return block[64:72], block[96:128]

    def rows_of(ref, blocks, start, size):
        return jnp.concatenate([ref[lb, start : start + size, :] for lb in range(blocks)], axis=1)

    def permute():
        for k in range(ROWS // SPAN):
            hi, lo = split(rows_of(state, 4, SPAN * k, SPAN))
            turned = mat(hi, order[...]) + mat(lo, order[...])
            for lb in range(4):
                state[lb, SPAN * k : SPAN * k + SPAN, :] = turned[:, 128 * lb : 128 * lb + 128]

    def transport(t):
        x_low = jnp.where(gx > 0, 1.0, 0.0).astype(F32)
        x_high = jnp.where(gx < GROUPS - 1, 1.0, 0.0).astype(F32)
        y_low = jnp.where(gy > 0, 1.0, 0.0).astype(F32)
        y_high = jnp.where(gy < OWNERS - 1, 1.0, 0.0).astype(F32)
        done = []
        for x in range(2):
            for y in range(2):
                center = faces[t, x, y]
                up = faces[t, 0, y] if x else halo[t, 0, y] * x_low
                down = halo[t, 1, y] * x_high if x else faces[t, 1, y]
                left = faces[t, x, 0] if y else halo[t, 2, x] * y_low
                right = halo[t, 3, x] * y_high if y else faces[t, x, 1]
                around = up + down + left + right
                around = around + pltpu.roll(center, 1, axis=1) + pltpu.roll(center, 127, axis=1)
                q = 2 * x + y
                done.append(center + 0.1 * (around - 6.0 * center) - speed[q : q + 1, :] * (center - up))
        return jnp.concatenate(done, axis=1)

    def chemistry(ref, blocks, keep, source, live):
        width = 128 * blocks
        wide = WIDE * 2 // blocks
        chains = range(CHAINS)

        def body(g, total):
            for c in chains:
                for i in range(wide):
                    p = (CHAINS * g + c) * wide + i
                    own = jnp.concatenate([ref[lb, pl.ds(p, NS, stride=NP), :] for lb in range(blocks)], axis=1)
                    feed[c * wide + i, 0:NS, 0:width] = own * keep + source[0:NS, 0:width]
            columns = [
                jnp.concatenate(
                    [
                        jnp.where(live > 0.5, feed[c * wide + i, :, 0:width], 0.0).astype(BF16)
                        for i in range(wide)
                    ],
                    axis=1,
                )
                for c in chains
            ]
            one = [silu(mat(weights_in, x)) for x in columns]
            two = [silu(mat(weights_hid, x)) for x in one]
            change = [mat(weights_out, x).astype(BF16).astype(F32) for x in two]
            for c in chains:
                for i in range(wide):
                    p = (CHAINS * g + c) * wide + i
                    part = jnp.where(live > 0.5, change[c][:, width * i : width * i + width], 0.0)
                    done = feed[c * wide + i, :, 0:width] + part
                    for lb in range(blocks):
                        ref[lb, pl.ds(p, NS, stride=NP), :] = done[0:NS, 128 * lb : 128 * lb + 128]
                    total = total + part
            return total

        return lax.fori_loop(0, NP // (CHAINS * wide), body, jnp.zeros((64, width), F32))

    def through(values, matrix, product=mat):
        hi, lo = split(values)
        both = product(jnp.concatenate([hi, lo], axis=0), matrix)
        return both[: values.shape[0]] + both[values.shape[0] :]

    for copy in loads[0:2]:
        copy.wait()
    for lb in range(2):
        mix(state, lb, partner[:, 128 * lb : 128 * lb + 128])
    row = iota((64, CELLS), 0)
    for t in range(2):
        if t == 1:
            await_cells(moved, 0, move_recv.at[0])
            await_cells(r_moved, 0, move_recv.at[2])
            meta, mate_of = unpack_cells(0)
            r_g[:, 0:128] = r_moved[0].reshape(DEVICES, 128).T[0:64]
            guest_keep, guest_live = 1.0 - meta[0:1], meta[1:2]
            guest_mates = mate_of.astype(jnp.int32)
            lands = (iota((CELLS, LIST), 0) == arrive[...]).astype(F32)
            taken = mat_nt(jnp.ones((8, LIST), BF16), lands.astype(BF16))[0:1]
            lands = lands.T
            for lb in range(4):
                turn[lb] = lands[:, 128 * lb : 128 * lb + 128]
            final[0:CELLS, :] = jnp.where(taken > 0.5, 0.0, order[...].astype(F32).T).astype(BF16)
            for c in range(2):
                final[CELLS + DEVICES * c : CELLS + DEVICES * (c + 1), :] = jnp.concatenate(
                    [turn[lb, pl.ds(c, DEVICES, stride=2), :] for lb in range(4)], axis=1
                ).astype(BF16)
        for copy in halos[t]:
            copy.wait_recv()
        grid = jnp.concatenate([transport(t), jnp.zeros((8, CELLS), F32)], axis=0)
        message = packed(to_box[...], jnp.where(row == LABEL, label_row, grid))
        for j in range(OWNERS):
            f_send[t, j] = message[HALF * j : HALF * j + HALF]
        exchange(f_send, f_recv, t, fs_sem, fr_sem)
        if t == 0:
            for copy in loads[2:4]:
                copy.wait()
            for lb in range(2, 4):
                mix(state, lb, partner[:, 128 * lb : 128 * lb + 128])
            permute()
            mates_now = mat(partner[...].astype(F32).astype(BF16), order[...])
            rate_row = through(jnp.broadcast_to(rate[...], (8, CELLS)), order[...])[0:1]
            keep_row = 1.0 - rate_row
            goes = (iota((CELLS, LIST), 0) == leave[...]).astype(F32)
            goes = mat(goes.T.astype(BF16), order[...])
            for lb in range(4):
                turn[lb] = goes[:, 128 * lb : 128 * lb + 128]
            for c in range(2):
                goes_halves[DEVICES * c : DEVICES * c + DEVICES, :] = jnp.concatenate(
                    [turn[lb, pl.ds(c, DEVICES, stride=2), :] for lb in range(4)], axis=1
                ).astype(BF16)
            live_all = jnp.concatenate([live_row, jnp.zeros((1, LIST), F32)], axis=1)
            extra = jnp.where(row == 0, rate_row, jnp.where(row == 1, live_all, 0.0))
            extra = jnp.concatenate([extra[0:32], mates_now], axis=0)
            mates[...] = extra
            pack_cells(0, goes_halves[0:DEVICES], extra)
            exchange_all(moving, moved, 0, 0, 1, EARLY)
        else:
            exchange_all(moving, moved, 1, 1, PACE[0], PACE[1])
            chemistry(guest, 1, guest_keep, r_g, guest_live)
            mix(guest, 0, guest_mates)
        await_row(f_recv, t, fr_sem)
        arrived = f_recv[t].reshape(PLACES // 2, 128)
        if t == 0:
            lane = iota((PLACES // 2, CELLS), 1).astype(F32) + 1.0
            for h in range(2):
                labels = arrived[:, 64 * h + LABEL : 64 * h + LABEL + 1]
                to_slot[h * PLACES // 2 : (h + 1) * PLACES // 2, :] = (labels == lane).astype(F32).astype(BF16)
        r_f[...] = through(unpacked(arrived, to_slot[...]), order[...]) * rate_row
        for lb in range(2):
            r_late[lb] = r_f[:, LIST + 128 * lb : LIST + 128 * lb + 128]
        hi, lo = split(r_f[...])
        both = mat_nt(goes_halves[...], jnp.concatenate([hi, lo], axis=0))
        both = both + pltpu.roll(both, 64, axis=1)
        r_moving[t, :, 0, :] = jnp.where(iota((DEVICES, 128), 1) < 64, both[:DEVICES], both[DEVICES:])
        if t == 1:
            exchange_all(r_moving, r_moved, 1, 3)
            exchange_all(moving, moved, 1, 1, PACE[1], DEVICES)
        total = chemistry(state, 2, keep_row[:, 0:LIST], r_f, live_row)
        source = through(total * (1.0 / NP), order[:, 0:LIST], mat_nt)
        message = packed(to_slot[...], source)
        for j in range(OWNERS):
            s_send[t, j] = message[HALF * j : HALF * j + HALF]
        exchange(s_send, s_recv, t, ss_sem, sr_sem)
        if t == 0:
            exchange_all(moving, moved, 0, 0, EARLY, DEVICES)
            exchange_all(r_moving, r_moved, 0, 2)
            for lb in range(4):
                cols = slice(128 * lb, 128 * lb + 128)
                mate_of = mates[32:64, cols].astype(jnp.int32)
                if lb < 2:
                    mix(state, lb, mate_of)
                else:
                    mix(state, lb, mate_of, keep_row[:, cols], lb - 2)
            pack_cells(1, goes_halves[DEVICES:], mates[...])
        else:
            def relax(s, carry):
                base = pl.multiple_of(s * NP, NP)
                for lb in range(2, 4):
                    cols = slice(128 * lb, 128 * lb + 128)
                    span = pl.ds(base, NP)
                    state[lb, span, :] = state[lb, span, :] * keep_row[:, cols] + r_late[lb - 2, pl.ds(s, 1), :]
                return carry

            lax.fori_loop(0, NS, relax, 0)
            for k in range(ROWS // SPAN):
                hi, lo = split(rows_of(state, 4, SPAN * k, SPAN))
                own = final[0:CELLS, :]
                made[SPAN * k : SPAN * k + SPAN, :] = mat(hi, own) + mat(lo, own)
            await_cells(moved, 1, move_recv.at[1])
            await_cells(r_moved, 1, move_recv.at[3])
            late_meta, _ = unpack_cells(1)
            r_turned = r_moved[1].reshape(DEVICES, 128).T
            r_g[...] = jnp.concatenate([r_turned[0:64], r_turned[64:128]], axis=1)
            guest_keep = jnp.concatenate([guest_keep, 1.0 - late_meta[0:1]], axis=1)
            guest_live = jnp.concatenate([guest_live, late_meta[1:2]], axis=1)
            chemistry(guest, 2, guest_keep, r_g, guest_live)

            stores = [
                pltpu.make_async_copy(
                    made.at[pl.ds(SPAN * k, SPAN)], parts_out.at[pl.ds(SPAN * k, SPAN)], store_sem.at[k]
                )
                for k in range(ROWS // SPAN)
            ]
            for k in range(ROWS // SPAN):
                hi, lo = split(rows_of(guest, 2, SPAN * k, SPAN))
                landing = final[CELLS:, :]
                made[SPAN * k : SPAN * k + SPAN, :] += mat(hi, landing) + mat(lo, landing)
                stores[k].start()
        await_row(s_recv, t, sr_sem)
        grid = grid + unpacked(s_recv[t].reshape(PLACES // 2, 128), to_box[...])
        if t == 0:
            for q in range(4):
                faces[1, q // 2, q % 2] = grid[0:56, 128 * q : 128 * q + 128]
            for copy in halos[1]:
                copy.start()
            exchange_all(moving, moved, 1, 1, 1, PACE[0])
        else:
            for q in range(4):
                grid_out[pl.ds(q, NS, stride=4), :] = grid[0:NS, 128 * q : 128 * q + 128]
    for copy in stores:
        copy.wait()
    for t in range(2):
        for copy in halos[t]:
            copy.wait_send()
        await_row(f_send, t, fs_sem)
        await_row(s_send, t, ss_sem)
        await_cells(moving, t, move_send.at[t])
        await_cells(r_moving, t, move_send.at[2 + t])


def per_device(
    grid_scalars, axial_speed, particles, cell_owner, cell_slot, mix_rate, partner,
    chem_input, chem_hidden, chem_output, react_slots, react_count, leave_slots, arrive_slots,
):
    vmem = pl.BlockSpec(memory_space=pltpu.VMEM)
    hbm = pl.BlockSpec(memory_space=pl.ANY)
    dma = pltpu.SemaphoreType.DMA
    messages = pltpu.VMEM((2, OWNERS, HALF, 128), F32)
    cells = pltpu.VMEM((2, DEVICES, 14, 128), F32)
    short = pltpu.VMEM((2, DEVICES, 1, 128), F32)
    grid, out = pl.pallas_call(
        step_kernel,
        out_shape=(
            jax.ShapeDtypeStruct((4 * NS, 128), F32),
            jax.ShapeDtypeStruct((ROWS, CELLS), F32),
        ),
        in_specs=[vmem, vmem, hbm] + [vmem] * 11,
        out_specs=(vmem, hbm),
        scratch_shapes=[
            pltpu.VMEM((4, ROWS, 128), F32),
            pltpu.VMEM((2, ROWS, 128), F32),
            pltpu.VMEM((2, 2, 2, 56, 128), F32),
            pltpu.VMEM((2, 4, 2, 56, 128), F32),
            messages,
            messages,
            messages,
            messages,
            cells,
            cells,
            short,
            short,
            pltpu.VMEM((PLACES, CELLS), BF16),
            pltpu.VMEM((PLACES, CELLS), BF16),
            pltpu.VMEM((CELLS, CELLS), BF16),
            pltpu.VMEM((CELLS + LIST, CELLS), BF16),
            pltpu.VMEM((4, LIST, 128), F32),
            pltpu.VMEM((LIST, CELLS), BF16),
            pltpu.VMEM((64, CELLS), F32),
            pltpu.VMEM((CHAINS * WIDE * 2, 64, LIST), F32),
            pltpu.VMEM((64, CELLS), F32),
            pltpu.VMEM((2, 64, 128), F32),
            pltpu.VMEM((64, LIST), F32),
            pltpu.VMEM((ROWS, CELLS), F32),
            pltpu.VMEM((128, 256), F32),
            pltpu.VMEM((64, 256), F32),
            dma((4,)),
            dma((ROWS // SPAN,)),
            dma((2, 4)),
            dma((2, 4)),
            dma((2,)),
            dma((2,)),
            dma((2,)),
            dma((2,)),
            dma((4,)),
            dma((4,)),
        ],
        compiler_params=pltpu.CompilerParams(
            collective_id=0, has_side_effects=True, vmem_limit_bytes=VMEM_LIMIT
        ),
        name="step",
    )(
        grid_scalars.reshape(4 * NS, 128),
        axial_speed.reshape(4, 128),
        particles.reshape(ROWS, CELLS),
        cell_owner.reshape(4, 128),
        cell_slot.reshape(4, 128),
        mix_rate.reshape(1, CELLS),
        partner,
        chem_input.T,
        chem_hidden,
        chem_output,
        react_slots,
        react_count.reshape(1, 1),
        leave_slots,
        arrive_slots,
    )
    return grid.reshape(grid_scalars.shape), out.reshape(particles.shape)


def solution(mesh):
    placed = (
        P(None, "gx", "gy", None),
        P("gx", "gy", None),
        P(None, None, ("gx", "gy")),
        P("gx", "gy", None),
        P("gx", "gy", None),
        P(("gx", "gy")),
        P(None, ("gx", "gy")),
        P(),
        P(),
        P(),
        P(("gx", "gy"), None),
        P(("gx", "gy")),
        P(("gx", "gy"), None),
        P(("gx", "gy"), None),
    )
    return jax.shard_map(
        per_device,
        mesh=mesh,
        in_specs=placed,
        out_specs=(P(None, "gx", "gy", None), P(None, None, ("gx", "gy"))),
        check_vma=False,
    )
```
